32 devices in a mesh: bf: 8 (over z, x), fr: 4 (over y, core).
Axes of the slice: x: 2, y: 2, z: 4, core: 2. Of those that a mesh axis runs over, the one named last changes fastest.
Arguments:
- top_source: bfloat16 [128, 4096], P('fr', 'bf'), may hold values from -6 to 6
- level_ordering: int32 [3, 8, 512], P(None, 'bf'), may hold values from 0 to 511, each once within a row
- butterfly_own: bfloat16 [3, 2048, 256], P(None, 'bf'), may hold values from -0.25 to 0.25
- butterfly_cross: bfloat16 [3, 2048, 256], P(None, 'bf'), may hold values from -0.25 to 0.25
- parent_rows: int32 [32, 256], P(('bf', 'fr')), may hold values from 0 to 511, as said below
- front_source: bfloat16 [128, 32768], P(None, ('bf', 'fr')), may hold values from -6 to 6
- panel_inverse: bfloat16 [32768, 1024], P(('bf', 'fr')), as said below
- coupling_read: bfloat16 [32768, 256], P(('bf', 'fr')), may hold values from -0.1875 to 0.1875
- coupling_write: bfloat16 [8192, 1024], P(('bf', 'fr')), may hold values from -0.25 to 0.25
Outputs:
- top_solution: bfloat16 [128, 4096], P('fr', 'bf')
- front_solution: bfloat16 [128, 32768], P(None, ('bf', 'fr'))
The draws below stay inside these ranges and needn't reach their ends.
Inputs may be any that keep to these rules, and one draw needn't show every extreme that they name: `level_ordering`: for each level and group, a permutation of the group's 512 columns. `parent_rows`: each row holds 256 different column numbers. `panel_inverse`: each panel's block is lower triangular: zero above its diagonal.
All inputs are finite; a program needn't handle non-finite values.
Results may differ from the reference program's by a relative error of at most 0.0057.
Values may be sent and summed in bfloat16 or wider, within the bound.
No kernel may reach another device: no remote copies, remote signals or barrier semaphores. Data moves between devices by JAX's collectives and lax.ppermute only.
A program may use at most 64 MiB of HBM per device.

```python
import jax
import jax.numpy as jnp
import numpy as np
from jax import lax

VECS = 128
BLK = 256
TOP_BLOCKS = 2
LEVELS = 3
PANEL = 1024
RANK = 256
TOP_ROWS = 512
GROUPS = 8
CHAIN = 4
NTOP = 4096
NLOW = 32768


def draw_parent_rows(key, part):
    base = jax.random.fold_in(key, 11)
    keys = jax.random.split(base, GROUPS * CHAIN)

    def pick(single):
        return jax.random.permutation(single, TOP_ROWS)[:RANK]
    return jax.vmap(pick)(keys).astype(jnp.int32)


def draw_panel_inverse(key, part):
    base = jax.random.fold_in(key, 23)
    keys = jax.random.split(base, GROUPS * CHAIN)
    lower_mask = jnp.tril(jnp.ones((PANEL, PANEL), jnp.float32), -1)
    identity = jnp.eye(PANEL, dtype=jnp.float32)

    def one_panel(single):
        key_spread, key_diagonal = jax.random.split(single)
        spread = jax.random.normal(key_spread, (PANEL, PANEL), jnp.float32)
        diagonal = jax.random.uniform(key_diagonal, (PANEL,), jnp.float32, 0.5, 1.5)
        matrix = spread * lower_mask * (1.0 / PANEL) ** 0.5 + identity * diagonal[None, :]
        return matrix.astype(jnp.bfloat16)
    return lax.map(one_panel, keys).reshape(GROUPS * CHAIN * PANEL, PANEL)


def block_levels(own_key, extent, cuts, low, largest):
    gain, own = 1.0, jax.random.fold_in(own_key, 6)
    for dim, parts in cuts:
        draws = jnp.exp(jax.random.uniform(jax.random.fold_in(own, dim), (parts,), jnp.float32, low / len(cuts), largest / len(cuts)))
        gain = gain * jnp.repeat(draws, extent[dim] // parts).reshape([-1 if axis == dim else 1 for axis in range(len(extent))])
    return gain


def noise(rng, extent, width, bound, cuts=(), held_as=jnp.bfloat16):
    drawn = width * jax.random.normal(rng, extent, jnp.float32)
    if cuts:
        drawn = drawn * block_levels(rng, extent, cuts, -0.22, 0.18)
    return jnp.clip(drawn, -bound, bound).astype(held_as)


def setup_inputs(seed: int = 0) -> dict:
    seeds = jax.random.split(jax.random.key(seed), 10)
    return {
        "top_source": noise(seeds[0], (VECS, NTOP), 1.0, 6.0, ((0, 4), (1, 8))),
        "level_ordering": jax.vmap(lambda own: jax.random.permutation(own, TOP_ROWS))(jax.random.split(seeds[1], LEVELS * GROUPS)).reshape((LEVELS, GROUPS, TOP_ROWS)).astype(jnp.int32),
        "butterfly_own": noise(seeds[2], (LEVELS, GROUPS * BLK, BLK), (2 * BLK) ** -0.5, 0.25, ((1, 8),)),
        "butterfly_cross": noise(seeds[3], (LEVELS, GROUPS * BLK, BLK), (2 * BLK) ** -0.5, 0.25, ((1, 8),)),
        "parent_rows": draw_parent_rows(jax.random.fold_in(seeds[9], 71), 0),
        "front_source": noise(seeds[5], (VECS, NLOW), 1.0, 6.0, ((1, 32),)),
        "panel_inverse": draw_panel_inverse(jax.random.fold_in(seeds[9], 71), 0),
        "coupling_read": noise(seeds[7], (GROUPS * CHAIN * PANEL, RANK), PANEL ** -0.5, 0.1875, ((0, 32),)),
        "coupling_write": noise(seeds[8], (GROUPS * CHAIN * RANK, PANEL), (2 * RANK) ** -0.5, 0.25, ((0, 32),)),
    }


def exact_dot(left, right):
    return jnp.dot(left.astype(jnp.float32), right.astype(jnp.float32), precision=lax.Precision.HIGHEST, preferred_element_type=jnp.float32)


def butterfly(top_source, level_ordering, butterfly_own, butterfly_cross):
    blocks_now = top_source.reshape(VECS, GROUPS, TOP_ROWS)
    for level_index in range(LEVELS):
        ordering = level_ordering[level_index].astype(jnp.int32)
        shuffled = jnp.take_along_axis(blocks_now, jnp.broadcast_to(ordering[None], blocks_now.shape), axis=2)
        partners = np.arange(GROUPS) ^ (1 << level_index)
        partner = shuffled[:, partners, :]
        own_factor = butterfly_own[level_index].reshape(GROUPS, BLK, BLK).astype(jnp.float32)
        cross_factor = butterfly_cross[level_index].reshape(GROUPS, BLK, BLK).astype(jnp.float32)
        left_part = shuffled.reshape(VECS, GROUPS, TOP_BLOCKS, BLK).astype(jnp.float32)
        right_part = partner.reshape(VECS, GROUPS, TOP_BLOCKS, BLK).astype(jnp.float32)
        combined = jnp.einsum("vgjr,grs->vgjs", left_part, own_factor) + jnp.einsum("vgjr,grs->vgjs", right_part, cross_factor)
        blocks_now = combined.astype(jnp.bfloat16).reshape(VECS, GROUPS, TOP_ROWS)
    return blocks_now


def chain_solve(inputs):
    top_group, row_picks, source, inverse, reader, writer = inputs

    def advance(incoming, pieces):
        picks, source_panel, inverse_panel, read_panel, write_panel = pieces
        linked = jnp.take(top_group, picks.astype(jnp.int32), axis=1)
        link_rank = exact_dot(incoming, read_panel) + linked.astype(jnp.float32)
        residue = source_panel.astype(jnp.float32) - exact_dot(link_rank, write_panel)
        solved = exact_dot(residue, inverse_panel)
        return solved, solved

    initial = jnp.zeros((VECS, PANEL), jnp.float32)
    _, solved_all = lax.scan(advance, initial, (row_picks, source, inverse, reader, writer))
    return solved_all.astype(jnp.bfloat16)


def reference(top_source, level_ordering, butterfly_own, butterfly_cross, parent_rows, front_source, panel_inverse, coupling_read, coupling_write):
    blocks_now = butterfly(top_source, level_ordering, butterfly_own, butterfly_cross)
    top_solution = blocks_now.reshape(VECS, NTOP)
    top_groups = jnp.transpose(blocks_now, (1, 0, 2))
    row_picks = parent_rows.reshape(GROUPS, CHAIN, RANK)
    source = jnp.transpose(front_source.reshape(VECS, GROUPS, CHAIN, PANEL), (1, 2, 0, 3))
    inverse = panel_inverse.reshape(GROUPS, CHAIN, PANEL, PANEL)
    reader = coupling_read.reshape(GROUPS, CHAIN, PANEL, RANK)
    writer = coupling_write.reshape(GROUPS, CHAIN, RANK, PANEL)
    solved = lax.map(chain_solve, (top_groups, row_picks, source, inverse, reader, writer))
    front_solution = jnp.transpose(solved, (2, 0, 1, 3)).reshape(VECS, NLOW)
    return (top_solution, front_solution)
```

```python
import jax
import jax.numpy as jnp
from jax import lax
from jax.sharding import PartitionSpec as P

BF16 = jnp.bfloat16


def dot(left, right):
    return jnp.dot(left, right, preferred_element_type=jnp.float32)


def swapped(value, axis, stride):
    mask = 2**stride
    pairs = [(source, source ^ mask) for source in range(lax.axis_size(axis))]
    return lax.ppermute(value, axis, pairs)


def moved(array, axis, by):
    devices = lax.axis_size(axis)
    pairs = [(i, i + by) for i in range(devices) if 0 <= i + by < devices]
    return lax.ppermute(array, axis, pairs)


def picker(columns, size):
    rows = lax.broadcasted_iota(jnp.int32, (size, columns.shape[0]), 0)
    return (rows == columns[None, :]).astype(BF16)


def doubled(factor, blocks):
    zero = jnp.zeros_like(factor)
    return jnp.concatenate(
        [
            jnp.concatenate([factor if i == j else zero for j in range(blocks)], axis=1)
            for i in range(blocks)
        ],
        axis=0,
    )


def body(
    top_source,
    level_ordering,
    butterfly_own,
    butterfly_cross,
    parent_rows,
    front_source,
    panel_inverse,
    coupling_read,
    coupling_write,
):
    level_count = level_ordering.shape[0]
    top_rows = top_source.shape[1]
    block_size = butterfly_own.shape[1]
    blocks = top_rows // block_size
    chain_length = lax.axis_size("fr")
    vectors = front_source.shape[0]
    rank = coupling_write.shape[0]

    next_read = moved(coupling_read, "fr", -1)

    pickers = [picker(level_ordering[level, 0], top_rows) for level in range(level_count)]

    def shuffled_factor(factor, level):
        if level + 1 == level_count:
            return doubled(factor, blocks)
        pieces = pickers[level + 1].reshape(blocks, block_size, top_rows)
        return jnp.concatenate(
            [dot(factor, pieces[j]).astype(BF16) for j in range(blocks)], axis=0
        )

    own = [shuffled_factor(butterfly_own[level], level) for level in range(level_count)]
    cross = [shuffled_factor(butterfly_cross[level], level) for level in range(level_count)]

    write_inverse = dot(coupling_write, panel_inverse).astype(BF16)
    source_inverse = dot(front_source, panel_inverse)

    shuffled = dot(top_source, pickers[0]).astype(BF16)
    for level in range(level_count):
        partner = swapped(shuffled, "bf", level)
        shuffled = (dot(shuffled, own[level]) + dot(partner, cross[level])).astype(BF16)
    top = shuffled

    carry = jnp.concatenate(
        [
            dot(source_inverse.astype(BF16), next_read).astype(BF16),
            dot(write_inverse, next_read).astype(BF16),
            jnp.broadcast_to((parent_rows // rank).astype(BF16), (8, rank)),
            jnp.broadcast_to((parent_rows % rank).astype(BF16), (8, rank)),
        ],
        axis=0,
    )
    state = jnp.zeros((vectors + top_rows, rank), jnp.float32)
    pad = jnp.zeros((vectors, rank), BF16)
    for distance in range(chain_length - 1, 0, -1):
        block = moved(carry, "fr", distance)
        base = block[:vectors].astype(jnp.float32)
        step = block[vectors : vectors + rank]
        high = block[vectors + rank].astype(jnp.int32)
        low = block[vectors + rank + 8].astype(jnp.int32)
        picks = picker(high * rank + low, top_rows)
        link = (state + jnp.concatenate([pad, picks], axis=0)).astype(BF16)
        mixed = dot(link, step)
        state = jnp.concatenate([base - mixed[:vectors], -mixed[vectors:]], axis=0)
    link = state + jnp.concatenate([pad, picker(parent_rows[0], top_rows)], axis=0)
    link = link.astype(BF16)
    fixed = source_inverse - dot(link[:vectors], write_inverse)
    reach = link[vectors:]

    rows = top.shape[0]
    place = lax.axis_index("fr")
    order = [(0, top)]
    for shift in range(1, chain_length):
        pairs = [(i, (i + shift) % chain_length) for i in range(chain_length)]
        order.append((shift, lax.ppermute(top, "fr", pairs)))
    whole = jnp.zeros((vectors, top_rows), BF16)
    for shift, piece in order:
        owner = lax.rem(place + chain_length - shift, chain_length)
        whole = lax.dynamic_update_slice(whole, piece, (owner * rows, 0))
    linked = dot(whole, reach).astype(BF16)
    solved = fixed - dot(linked, write_inverse)
    return (top, solved.astype(BF16))


def solution(mesh):
    placed = (
        P("fr", "bf"),
        P(None, "bf", None),
        P(None, "bf", None),
        P(None, "bf", None),
        P(("bf", "fr"), None),
        P(None, ("bf", "fr")),
        P(("bf", "fr"), None),
        P(("bf", "fr"), None),
        P(("bf", "fr"), None),
    )
    return jax.shard_map(
        body,
        mesh=mesh,
        in_specs=placed,
        out_specs=(P("fr", "bf"), P(None, ("bf", "fr"))),
        check_vma=False,
    )
```

```python
import functools

import jax
import jax.numpy as jnp
from jax import lax
from jax.experimental import pallas as pl
from jax.experimental.pallas import tpu as pltpu
from jax.sharding import PartitionSpec as P

BF16 = jnp.bfloat16
F32 = jnp.float32
LOW_BITS = 8
INDEX_ROWS = 16


def dot(left, right):
    return jnp.dot(left, right, preferred_element_type=F32)


def picker(columns, size):
    rows = lax.broadcasted_iota(jnp.int32, (size, columns.shape[1]), 0)
    return jnp.where(rows == columns, 1.0, 0.0).astype(BF16)


def kernel_call(kernel, outs, scratch, operands, flops=0, after=()):
    taken = len(operands)
    operands = [*operands, *after]

    def run(*refs):
        kernel(*refs[:taken], *refs[len(operands) :])

    vmem = pl.BlockSpec(memory_space=pltpu.VMEM)
    shapes = [
        pltpu.VMEM(shape, dtype) if inside else jax.ShapeDtypeStruct(shape, dtype)
        for shape, dtype, inside in outs
    ]
    placed = [pltpu.with_memory_space_constraint(x, pltpu.VMEM) for x in operands]
    return pl.pallas_call(
        run,
        out_shape=shapes,
        in_specs=[vmem] * len(placed),
        out_specs=[vmem] * len(shapes),
        scratch_shapes=scratch,
        compiler_params=pltpu.CompilerParams(vmem_limit_bytes=24 * 1024 * 1024),
        cost_estimate=pl.CostEstimate(flops=flops, bytes_accessed=0, transcendentals=0),
    )(*placed)


def pickers_kernel(order_ref, pick_ref):
    for level in range(pick_ref.shape[0]):
        pick_ref[level] = picker(order_ref[level], pick_ref.shape[1])


def panel_kernel(write_ref, inverse_ref, source_ref, gain_ref, base_ref):
    inverse = inverse_ref[...]
    gain_ref[...] = dot(write_ref[...], inverse).astype(BF16)
    base_ref[...] = dot(source_ref[...], inverse)


def block_kernel(gain_ref, base_ref, read_ref, rows_ref, block_ref):
    vectors, rank = base_ref.shape[0], gain_ref.shape[0]
    read = read_ref[...]
    block_ref[:vectors] = dot(base_ref[...].astype(BF16), read).astype(BF16)
    block_ref[vectors : vectors + rank] = dot(gain_ref[...], read).astype(BF16)
    rows = rows_ref[...]
    low = jnp.bitwise_and(rows, 2**LOW_BITS - 1)
    high = lax.shift_right_logical(rows, jnp.full(rows.shape, LOW_BITS, jnp.int32))
    at = vectors + rank
    for part in (low, high):
        wide = jnp.broadcast_to(part.astype(F32), (INDEX_ROWS, rank))
        block_ref[at : at + INDEX_ROWS] = wide.astype(BF16)
        at += INDEX_ROWS


def mixed(own_part, partner_part, own, cross):
    size = own.shape[0]
    pieces = []
    for start in range(0, own_part.shape[1], size):
        cut = slice(start, start + size)
        pieces.append(dot(own_part[:, cut], own) + dot(partner_part[:, cut], cross))
    return jnp.concatenate(pieces, axis=1)


def first_kernel(chips, pick_ref, order_ref, own_ref, cross_ref, *refs):
    slabs, partners, (out_ref, held, swap) = refs[:chips], refs[chips : 2 * chips], refs[2 * chips :]
    rows, size = slabs[0].shape
    chip = lax.axis_index("fr") // 2
    partner_pick = picker(order_ref[0], size)
    for shift in range(chips):
        slot = pl.ds(pl.multiple_of(lax.rem(chip + chips - shift, chips) * rows, rows), rows)
        held[slot, :] = dot(slabs[shift][...], pick_ref[0])
        swap[slot, :] = dot(partners[shift][...], partner_pick)
    level = mixed(held[...].astype(BF16), swap[...].astype(BF16), own_ref[0], cross_ref[0])
    out_ref[...] = dot(level.astype(BF16), pick_ref[1]).astype(BF16)


def level_kernel(level, pick_ref, own_ref, cross_ref, held_ref, swap_ref, out_ref):
    mix = mixed(held_ref[...], swap_ref[...], own_ref[level], cross_ref[level])
    out_ref[...] = dot(mix.astype(BF16), pick_ref[level + 1]).astype(BF16)


def chain_kernel(
    gain_ref, base_ref, block_ref, other_ref, fixed_ref, reach_ref, slope_ref, hop_fixed_ref, hop_ref, *hop_slope
):
    vectors, rank = base_ref.shape[0], gain_ref.shape[0]
    top_rows = hop_ref.shape[0]
    odd = lax.rem(lax.axis_index("fr"), 2) == 1

    def parts(ref):
        at = vectors + rank
        low = ref[at : at + INDEX_ROWS].astype(F32)[:1].astype(jnp.int32)
        at += INDEX_ROWS
        high = ref[at : at + INDEX_ROWS].astype(F32)[:1].astype(jnp.int32)
        return ref[:vectors], ref[vectors : vectors + rank], high * 2**LOW_BITS + low

    base_own, step_own, rows_own = parts(block_ref)
    base_other, step_other, rows_other = parts(other_ref)
    base_even = jnp.where(odd, base_other, base_own)
    base_odd = jnp.where(odd, base_own, base_other)
    step_even = jnp.where(odd, step_other, step_own)
    step_odd = jnp.where(odd, step_own, step_other)
    pick_even = picker(jnp.where(odd, rows_other, rows_own), top_rows)
    pick_odd = picker(jnp.where(odd, rows_own, rows_other), top_rows)

    past = (dot(pick_even, step_even) - pick_odd.astype(F32)).astype(BF16)
    hop_fixed_ref[...] = base_odd.astype(F32) - dot(base_even, step_odd)
    hop_ref[...] = dot(past, step_odd).astype(BF16)
    for ref in hop_slope:
        ref[...] = dot(step_even, step_odd).astype(BF16)
    reach_ref[...] = jnp.where(odd, -past, pick_even)
    gain = gain_ref[...]
    fixed_ref[...] = base_ref[...] - dot(jnp.where(odd, base_even, jnp.zeros_like(base_even)), gain)
    slope_ref[...] = jnp.where(odd, -dot(step_even, gain), gain.astype(F32)).astype(BF16)


def last_kernel(
    chips, level, own_ref, cross_ref, held_ref, swap_ref, hop_fixed_ref, hop_ref, top_ref, pass_ref, out_ref, wide
):
    rows = out_ref.shape[0]
    place = lax.axis_index("fr")
    mix = mixed(held_ref[...], swap_ref[...], own_ref[level], cross_ref[level])
    wide[...] = mix
    top = mix.astype(BF16)
    top_ref[...] = top
    out_ref[...] = wide[pl.ds(pl.multiple_of(place // 2 * rows, rows), rows), :].astype(BF16)
    moved = dot(top, hop_ref[...])
    for chip in range(chips):
        start = pl.multiple_of((2 * chip + lax.rem(place, 2)) * rows, rows)
        cut = slice(chip * rows, (chip + 1) * rows)
        wide[cut, : moved.shape[1]] = moved[cut] + hop_fixed_ref[pl.ds(start, rows), :]
    pass_ref[...] = wide[:, : moved.shape[1]].astype(BF16)


def in_order(wide, own, other, rows):
    core = lax.rem(lax.axis_index("fr"), 2)
    for chip in range(own.shape[0] // rows):
        cut = slice(chip * rows, (chip + 1) * rows)
        for piece, side in ((own, core), (other, 1 - core)):
            wide[pl.ds(pl.multiple_of((2 * chip + side) * rows, rows), rows), :] = piece[cut]
    return wide[...]


def link_kernel(rows, fixed_ref, reach_ref, gain_ref, top_ref, other_ref, out_ref, wide):
    reach = reach_ref[...]
    link = in_order(wide, dot(top_ref[...], reach), dot(other_ref[...], reach), rows)
    out_ref[...] = fixed_ref[...] - dot(link.astype(BF16), gain_ref[...])


def final_kernel(rows, fixed_ref, slope_ref, own_ref, other_ref, out_ref, wide):
    arrived = in_order(wide, own_ref[...].astype(F32), other_ref[...].astype(F32), rows)
    arrived = jnp.where(lax.axis_index("fr") >= 2, arrived, 0.0).astype(BF16)
    out_ref[...] = (fixed_ref[...] - dot(arrived, slope_ref[...])).astype(BF16)


def body(
    top_source,
    level_ordering,
    butterfly_own,
    butterfly_cross,
    parent_rows,
    front_source,
    panel_inverse,
    coupling_read,
    coupling_write,
):
    levels = level_ordering.shape[0]
    rows, top_rows = top_source.shape
    vectors, panel = front_source.shape
    rank = coupling_write.shape[0]
    groups, chain = lax.axis_size("bf"), lax.axis_size("fr")
    chips = chain // 2
    local = rows * chips

    def turned(array, by, flip=0):
        pairs = [(i, (i + by) % chain ^ flip) for i in range(chain)]
        return lax.ppermute(array, "fr", pairs)

    def swapped(array, bit, by=0):
        if not by:
            return lax.ppermute(array, "bf", [(g, g ^ bit) for g in range(groups)])
        pairs = [
            (g * chain + i, (g ^ bit) * chain + (i + by) % chain)
            for g in range(groups)
            for i in range(chain)
        ]
        return lax.ppermute(array, ("bf", "fr"), pairs)

    partner_order = swapped(level_ordering, 1)
    slabs = [top_source] + [turned(top_source, 2 * shift) for shift in range(1, chips)]
    partners = [swapped(top_source, 1, 2 * shift) for shift in range(chips)]
    next_read = turned(coupling_read, -1)

    (pick,) = kernel_call(
        pickers_kernel, [((levels, top_rows, top_rows), BF16, True)], [], [level_ordering]
    )
    gain, base = kernel_call(
        panel_kernel,
        [((rank, panel), BF16, True), ((vectors, panel), F32, True)],
        [],
        [coupling_write, panel_inverse, front_source],
        2 * (rank + vectors) * panel * panel,
    )

    wide = pltpu.VMEM((local, top_rows), F32)
    factors = [butterfly_own, butterfly_cross]
    (held,) = kernel_call(
        functools.partial(first_kernel, chips),
        [((local, top_rows), BF16, True)],
        [wide, wide],
        [pick, partner_order, *factors, *slabs, *partners],
    )
    for level in range(1, levels - 1):
        swap = swapped(held, 2**level)
        (held,) = kernel_call(
            functools.partial(level_kernel, level),
            [((local, top_rows), BF16, True)],
            [],
            [pick, *factors, held, swap],
        )
    swap = swapped(held, 2 ** (levels - 1))

    (block,) = kernel_call(
        block_kernel,
        [((vectors + rank + 2 * INDEX_ROWS, rank), BF16, True)],
        [],
        [gain, base, next_read, parent_rows],
        2 * (vectors + rank) * panel * rank,
        [held],
    )
    other = turned(block, 0, 1)
    outs = [
        ((vectors, panel), F32, True),
        ((top_rows, rank), BF16, True),
        ((rank, panel), BF16, True),
        ((vectors, rank), F32, True),
        ((top_rows, rank), BF16, True),
    ] + [((rank, rank), BF16, True)] * (chips > 2)
    fixed, reach, slope, hop_fixed, hop, *hop_slope = kernel_call(
        chain_kernel, outs, [], [gain, base, block, other], 2 * rank * rank * panel
    )

    top, passed, top_own = kernel_call(
        functools.partial(last_kernel, chips, levels - 1),
        [
            ((local, top_rows), BF16, True),
            ((local, rank), BF16, True),
            ((rows, top_rows), BF16, False),
        ],
        [wide],
        [*factors, held, swap, hop_fixed, hop],
    )
    start = passed
    for _ in range(chips - 2):
        here = jnp.where(lax.axis_index("fr") >= 2, turned(passed, 2), 0)
        passed = (start.astype(F32) + dot(here, hop_slope[0])).astype(BF16)
    arrived_cross = turned(passed, 2, 1)
    arrived = turned(passed, 2)
    top_other = turned(top, 0, 1)
    (ready,) = kernel_call(
        functools.partial(link_kernel, rows),
        [((vectors, panel), F32, True)],
        [pltpu.VMEM((vectors, rank), F32)],
        [fixed, reach, gain, top, top_other],
    )
    (solved,) = kernel_call(
        functools.partial(final_kernel, rows),
        [((vectors, panel), BF16, False)],
        [pltpu.VMEM((vectors, rank), F32)],
        [ready, slope, arrived, arrived_cross],
    )
    return (top_own, solved)


def solution(mesh):
    placed = (
        P("fr", "bf"),
        P(None, "bf", None),
        P(None, "bf", None),
        P(None, "bf", None),
        P(("bf", "fr"), None),
        P(None, ("bf", "fr")),
        P(("bf", "fr"), None),
        P(("bf", "fr"), None),
        P(("bf", "fr"), None),
    )
    return jax.shard_map(
        body,
        mesh=mesh,
        in_specs=placed,
        out_specs=(P("fr", "bf"), P(None, ("bf", "fr"))),
        check_vma=False,
    )
```

```python
import functools

import jax
import jax.numpy as jnp
from jax import lax
from jax.experimental import pallas as pl
from jax.experimental.pallas import tpu as pltpu
from jax.sharding import PartitionSpec as P

BF16 = jnp.bfloat16
F32 = jnp.float32
LOW_BITS = 8
INDEX_ROWS = 16
LEVEL_COST = 4 * 10**9


def dot(left, right):
    return jnp.dot(left, right, preferred_element_type=F32)


def picker(columns, size):
    rows = lax.broadcasted_iota(jnp.int32, (size, columns.shape[1]), 0)
    return jnp.where(rows == columns, 1.0, 0.0).astype(BF16)


def kernel_call(kernel, outs, scratch, operands, flops=0, remote=()):
    vmem, hbm = pl.BlockSpec(memory_space=pltpu.VMEM), pl.BlockSpec(memory_space=pltpu.HBM)
    shapes = [
        pltpu.VMEM(shape, dtype) if inside else jax.ShapeDtypeStruct(shape, dtype)
        for shape, dtype, inside in outs
    ]
    placed = [pltpu.with_memory_space_constraint(x, pltpu.VMEM) for x in operands]
    return pl.pallas_call(
        kernel,
        out_shape=shapes,
        in_specs=[vmem] * len(placed) + [hbm] * len(remote),
        out_specs=[vmem if inside else hbm for _, _, inside in outs],
        scratch_shapes=scratch,
        compiler_params=pltpu.CompilerParams(vmem_limit_bytes=24 * 1024 * 1024),
        cost_estimate=pl.CostEstimate(flops=flops, bytes_accessed=0, transcendentals=0),
    )(*placed, *[pltpu.with_memory_space_constraint(x, pltpu.HBM) for x in remote])


def shuffle_kernel(source_hbm, order_hbm, own_hbm, cross_hbm, out_ref, order_ref, own_ref, cross_ref, source, sems):
    pairs = [(order_hbm, order_ref), (source_hbm, source), (own_hbm, own_ref), (cross_hbm, cross_ref)]
    copies = [pltpu.make_async_copy(a, b, sems.at[i]) for i, (a, b) in enumerate(pairs)]
    for copy in copies:
        copy.start()
    copies[0].wait()
    pick = picker(order_ref[0], source.shape[1])
    copies[1].wait()
    out_ref[...] = dot(source[...], pick).astype(BF16)
    copies[2].wait()
    copies[3].wait()


def panel_kernel(order_ref, write_hbm, inverse_hbm, source_hbm, gain_ref, base_ref, pick_ref, left, inverse, sems):
    rank, size = gain_ref.shape
    part = rank
    copies = [
        pltpu.make_async_copy(write_hbm, left.at[:rank], sems.at[0]),
        pltpu.make_async_copy(source_hbm, left.at[rank:], sems.at[1]),
    ]
    for start in range(0, size, part):
        block = (pl.ds(start, part), pl.ds(0, start + part))
        copies.append(
            pltpu.make_async_copy(inverse_hbm.at[block], inverse.at[block], sems.at[2 + start // part])
        )
    for copy in copies:
        copy.start()
    for level in range(pick_ref.shape[0]):
        pick_ref[level] = picker(order_ref[level + 1], pick_ref.shape[1])
    for copy in copies:
        copy.wait()
    for start in range(0, size, part):
        cut = slice(start, start + part)
        product = dot(left[:, start:], inverse[start:, cut])
        gain_ref[:, cut] = product[:rank].astype(BF16)
        base_ref[:, cut] = product[rank:]


def block_kernel(gain_ref, base_ref, read_ref, rows_ref, block_ref):
    vectors, rank = base_ref.shape[0], gain_ref.shape[0]
    read = read_ref[...]
    block_ref[:vectors] = dot(base_ref[...].astype(BF16), read).astype(BF16)
    block_ref[vectors : vectors + rank] = dot(gain_ref[...], read).astype(BF16)
    rows = rows_ref[...]
    low = jnp.bitwise_and(rows, 2**LOW_BITS - 1)
    high = lax.shift_right_logical(rows, jnp.full(rows.shape, LOW_BITS, jnp.int32))
    at = vectors + rank
    for part in (low, high):
        wide = jnp.broadcast_to(part.astype(F32), (INDEX_ROWS, rank))
        block_ref[at : at + INDEX_ROWS] = wide.astype(BF16)
        at += INDEX_ROWS


def mixed(own_part, partner_part, own, cross):
    size = own.shape[0]
    pieces = []
    for start in range(0, own_part.shape[1], size):
        cut = slice(start, start + size)
        pieces.append(dot(own_part[:, cut], own) + dot(partner_part[:, cut], cross))
    return jnp.concatenate(pieces, axis=1)


def level_kernel(level, pick_ref, own_ref, cross_ref, held_ref, swap_ref, out_ref):
    mix = mixed(held_ref[...], swap_ref[...], own_ref[level], cross_ref[level])
    out_ref[...] = dot(mix.astype(BF16), pick_ref[level]).astype(BF16)


def chain_kernel(
    gain_ref, base_ref, block_ref, other_ref, fixed_ref, reach_ref, slope_ref, hop_fixed_ref, hop_ref, *hop_slope
):
    vectors, rank = base_ref.shape[0], gain_ref.shape[0]
    top_rows = hop_ref.shape[0]
    odd = lax.rem(lax.axis_index("fr"), 2) == 1

    def parts(ref):
        at = vectors + rank
        low = ref[at : at + INDEX_ROWS].astype(F32)[:1].astype(jnp.int32)
        at += INDEX_ROWS
        high = ref[at : at + INDEX_ROWS].astype(F32)[:1].astype(jnp.int32)
        return ref[:vectors], ref[vectors : vectors + rank], high * 2**LOW_BITS + low

    base_own, step_own, rows_own = parts(block_ref)
    base_other, step_other, rows_other = parts(other_ref)
    base_even = jnp.where(odd, base_other, base_own)
    base_odd = jnp.where(odd, base_own, base_other)
    step_even = jnp.where(odd, step_other, step_own)
    step_odd = jnp.where(odd, step_own, step_other)
    pick_even = picker(jnp.where(odd, rows_other, rows_own), top_rows)
    pick_odd = picker(jnp.where(odd, rows_own, rows_other), top_rows)

    past = (dot(pick_even, step_even) - pick_odd.astype(F32)).astype(BF16)
    hop_fixed_ref[...] = base_odd.astype(F32) - dot(base_even, step_odd)
    hop_ref[...] = dot(past, step_odd).astype(BF16)
    for ref in hop_slope:
        ref[...] = dot(step_even, step_odd).astype(BF16)
    reach_ref[...] = jnp.where(odd, -past, pick_even)
    gain = gain_ref[...]
    fixed_ref[...] = base_ref[...] - dot(jnp.where(odd, base_even, jnp.zeros_like(base_even)), gain)
    slope_ref[...] = jnp.where(odd, -dot(step_even, gain), gain.astype(F32)).astype(BF16)


def last_kernel(level, own_ref, cross_ref, held_ref, swap_ref, top_ref):
    top_ref[...] = mixed(held_ref[...], swap_ref[...], own_ref[level], cross_ref[level]).astype(BF16)


def pass_kernel(hop_fixed_ref, hop_ref, *refs):
    *slabs, top_ref, pass_ref, wide = refs
    rows = slabs[0].shape[0]
    place = lax.axis_index("fr")
    for flip, slab in enumerate(slabs):
        start = pl.multiple_of(jnp.bitwise_xor(place, flip) * rows, rows)
        wide[pl.ds(start, rows), :] = slab[...].astype(F32)
    top = wide[...].astype(BF16)
    top_ref[...] = top
    pass_ref[...] = (hop_fixed_ref[...] + dot(top, hop_ref[...])).astype(BF16)


def link_kernel(fixed_ref, reach_ref, gain_ref, top_ref, out_ref):
    link = dot(top_ref[...], reach_ref[...]).astype(BF16)
    out_ref[...] = fixed_ref[...] - dot(link, gain_ref[...])


def final_kernel(fixed_ref, slope_ref, arrived_ref, top_ref, out_hbm, top_hbm, held, sems):
    first = pltpu.make_async_copy(top_ref, top_hbm, sems.at[0])
    first.start()
    arrived = jnp.where(lax.axis_index("fr") >= 2, arrived_ref[...].astype(F32), 0.0).astype(BF16)
    parts = sems.shape[0] - 1
    width = held.shape[1] // parts
    copies = [first]
    for part in range(parts):
        cut = pl.ds(part * width, width)
        held[:, cut] = (fixed_ref[:, cut] - dot(arrived, slope_ref[:, cut])).astype(BF16)
        copies.append(pltpu.make_async_copy(held.at[:, cut], out_hbm.at[:, cut], sems.at[part + 1]))
        copies[-1].start()
    for copy in copies:
        copy.wait()


def body(
    top_source,
    level_ordering,
    butterfly_own,
    butterfly_cross,
    parent_rows,
    front_source,
    panel_inverse,
    coupling_read,
    coupling_write,
):
    levels = level_ordering.shape[0]
    rows, top_rows = top_source.shape
    vectors, panel = front_source.shape
    rank = coupling_write.shape[0]
    groups, chain = lax.axis_size("bf"), lax.axis_size("fr")
    chips = chain // 2

    def flipped(array, mask):
        return lax.ppermute(array, "fr", [(i, i ^ mask) for i in range(chain)])

    def turned(array, by):
        return lax.ppermute(array, "fr", [(i, (i + by) % chain) for i in range(chain)])

    def swapped(array, mask):
        return lax.ppermute(array, "bf", [(g, g ^ mask) for g in range(groups)])

    held, order, own, cross = kernel_call(
        shuffle_kernel,
        [
            ((rows, top_rows), BF16, True),
            (level_ordering.shape, jnp.int32, True),
            (butterfly_own.shape, BF16, True),
            (butterfly_cross.shape, BF16, True),
        ],
        [pltpu.VMEM((rows, top_rows), BF16), pltpu.SemaphoreType.DMA((4,))],
        [],
        remote=[top_source, level_ordering, butterfly_own, butterfly_cross],
    )
    swap = swapped(held, 1)
    gain, base, pick = kernel_call(
        panel_kernel,
        [
            ((rank, panel), BF16, True),
            ((vectors, panel), F32, True),
            ((levels - 1, top_rows, top_rows), BF16, True),
        ],
        [
            pltpu.VMEM((rank + vectors, panel), BF16),
            pltpu.VMEM((panel, panel), BF16),
            pltpu.SemaphoreType.DMA((2 + panel // rank,)),
        ],
        [order],
        2 * (rank + vectors) * panel * panel,
        [coupling_write, panel_inverse, front_source],
    )
    coupling_read, gain = lax.optimization_barrier((coupling_read, gain))
    next_read = turned(coupling_read, -1)

    for level in range(levels - 1):
        (held,) = kernel_call(
            functools.partial(level_kernel, level),
            [((rows, top_rows), BF16, True)],
            [],
            [pick, own, cross, held, swap],
            LEVEL_COST,
        )
        swap = swapped(held, 2 ** (level + 1))

    next_read, held = lax.optimization_barrier((next_read, held))
    (block,) = kernel_call(
        block_kernel,
        [((vectors + rank + 2 * INDEX_ROWS, rank), BF16, True)],
        [],
        [gain, base, next_read, parent_rows],
        2 * (vectors + rank) * panel * rank,
    )
    other = flipped(block, 1)
    outs = [
        ((vectors, panel), F32, True),
        ((top_rows, rank), BF16, True),
        ((rank, panel), BF16, True),
        ((vectors, rank), F32, True),
        ((top_rows, rank), BF16, True),
    ] + [((rank, rank), BF16, True)] * (chips > 2)
    fixed, reach, slope, hop_fixed, hop, *hop_slope = kernel_call(
        chain_kernel, outs, [], [gain, base, block, other], 2 * rank * rank * panel
    )

    (top,) = kernel_call(
        functools.partial(last_kernel, levels - 1),
        [((rows, top_rows), BF16, True)],
        [],
        [own, cross, held, swap],
    )
    slabs = [top] + [flipped(top, mask) for mask in range(1, chain)]
    whole, passed = kernel_call(
        pass_kernel,
        [((vectors, top_rows), BF16, True), ((vectors, rank), BF16, True)],
        [pltpu.VMEM((vectors, top_rows), F32)],
        [hop_fixed, hop, *slabs],
    )
    start = passed
    for _ in range(chips - 2):
        here = jnp.where(lax.axis_index("fr") >= 2, turned(passed, 2), 0)
        passed = (start.astype(F32) + dot(here, hop_slope[0])).astype(BF16)
    arrived = turned(passed, 2)
    (ready,) = kernel_call(
        link_kernel, [((vectors, panel), F32, True)], [], [fixed, reach, gain, whole]
    )
    solved, top = kernel_call(
        final_kernel,
        [((vectors, panel), BF16, False), ((rows, top_rows), BF16, False)],
        [pltpu.VMEM((vectors, panel), BF16), pltpu.SemaphoreType.DMA((5,))],
        [ready, slope, arrived, top],
    )
    return (top, solved)


def solution(mesh):
    placed = (
        P("fr", "bf"),
        P(None, "bf", None),
        P(None, "bf", None),
        P(None, "bf", None),
        P(("bf", "fr"), None),
        P(None, ("bf", "fr")),
        P(("bf", "fr"), None),
        P(("bf", "fr"), None),
        P(("bf", "fr"), None),
    )
    return jax.shard_map(
        body,
        mesh=mesh,
        in_specs=placed,
        out_specs=(P("fr", "bf"), P(None, ("bf", "fr"))),
        check_vma=False,
    )
```

```python
import functools

import jax
import jax.numpy as jnp
from jax import lax
from jax.experimental import pallas as pl
from jax.experimental.pallas import tpu as pltpu
from jax.sharding import PartitionSpec as P

BF16 = jnp.bfloat16
F32 = jnp.float32
LOW_BITS = 8
INDEX_ROWS = 16
PANEL_COST = 10**9
LEVEL_COST = 4 * 10**9

def dot(left, right):
    return jnp.dot(left, right, preferred_element_type=F32)


def picker(columns, size):
    rows = lax.broadcasted_iota(jnp.int32, (size, columns.shape[1]), 0)
    return jnp.where(rows == columns, 1.0, 0.0).astype(BF16)


def kernel_call(kernel, outs, scratch, operands, flops=0, remote=()):
    vmem, hbm = pl.BlockSpec(memory_space=pltpu.VMEM), pl.BlockSpec(memory_space=pltpu.HBM)
    shapes = [
        pltpu.VMEM(shape, dtype) if inside else jax.ShapeDtypeStruct(shape, dtype)
        for shape, dtype, inside in outs
    ]
    placed = [pltpu.with_memory_space_constraint(x, pltpu.VMEM) for x in operands]
    return pl.pallas_call(
        kernel,
        out_shape=shapes,
        in_specs=[vmem] * len(placed) + [hbm] * len(remote),
        out_specs=[vmem if inside else hbm for _, _, inside in outs],
        scratch_shapes=scratch,
        compiler_params=pltpu.CompilerParams(vmem_limit_bytes=24 * 1024 * 1024),
        cost_estimate=pl.CostEstimate(flops=flops, bytes_accessed=0, transcendentals=0),
    )(*placed, *[pltpu.with_memory_space_constraint(x, pltpu.HBM) for x in remote])


def shuffle_kernel(source_hbm, order_hbm, own_hbm, cross_hbm, out_ref, order_ref, own_ref, cross_ref, source, sems):
    pairs = [(order_hbm, order_ref), (source_hbm, source), (own_hbm, own_ref), (cross_hbm, cross_ref)]
    copies = [pltpu.make_async_copy(a, b, sems.at[i]) for i, (a, b) in enumerate(pairs)]
    for copy in copies:
        copy.start()
    copies[0].wait()
    pick = picker(order_ref[0], source.shape[1])
    copies[1].wait()
    out_ref[...] = dot(source[...], pick).astype(BF16)
    copies[2].wait()
    copies[3].wait()


def pick_kernel(order_ref, pick_ref):
    for level in range(pick_ref.shape[0]):
        pick_ref[level] = picker(order_ref[level + 1], pick_ref.shape[1])


def panel_kernel(write_hbm, inverse_hbm, source_hbm, gain_ref, base_ref, left, inverse, sems):
    rank, size = gain_ref.shape
    part = rank
    copies = [
        pltpu.make_async_copy(write_hbm, left.at[:rank], sems.at[0]),
        pltpu.make_async_copy(source_hbm, left.at[rank:], sems.at[1]),
    ]
    for start in range(0, size, part):
        block = (pl.ds(start, part), pl.ds(0, start + part))
        copies.append(
            pltpu.make_async_copy(inverse_hbm.at[block], inverse.at[block], sems.at[2 + start // part])
        )
    for copy in copies:
        copy.start()
    for copy in copies:
        copy.wait()
    for start in range(0, size, part):
        cut = slice(start, start + part)
        product = dot(left[:, start:], inverse[start:, cut])
        gain_ref[:, cut] = product[:rank].astype(BF16)
        base_ref[:, cut] = product[rank:]


def block_kernel(gain_ref, base_ref, read_ref, rows_ref, block_ref):
    vectors, rank = base_ref.shape[0], gain_ref.shape[0]
    read = read_ref[...]
    block_ref[:vectors] = dot(base_ref[...].astype(BF16), read).astype(BF16)
    block_ref[vectors : vectors + rank] = dot(gain_ref[...], read).astype(BF16)
    rows = rows_ref[...]
    low = jnp.bitwise_and(rows, 2**LOW_BITS - 1)
    high = lax.shift_right_logical(rows, jnp.full(rows.shape, LOW_BITS, jnp.int32))
    at = vectors + rank
    for part in (low, high):
        wide = jnp.broadcast_to(part.astype(F32), (INDEX_ROWS, rank))
        block_ref[at : at + INDEX_ROWS] = wide.astype(BF16)
        at += INDEX_ROWS


def mixed(own_part, partner_part, own, cross):
    size = own.shape[0]
    pieces = []
    for start in range(0, own_part.shape[1], size):
        cut = slice(start, start + size)
        pieces.append(dot(own_part[:, cut], own) + dot(partner_part[:, cut], cross))
    return jnp.concatenate(pieces, axis=1)


def level_kernel(level, pick_ref, own_ref, cross_ref, held_ref, swap_ref, out_ref):
    mix = mixed(held_ref[...], swap_ref[...], own_ref[level], cross_ref[level])
    out_ref[...] = dot(mix.astype(BF16), pick_ref[level]).astype(BF16)


def chain_kernel(
    gain_ref, base_ref, block_ref, other_ref, fixed_ref, reach_ref, slope_ref, hop_fixed_ref, hop_ref, *hop_slope
):
    vectors, rank = base_ref.shape[0], gain_ref.shape[0]
    top_rows = hop_ref.shape[0]
    odd = lax.rem(lax.axis_index("fr"), 2) == 1

    def parts(ref):
        at = vectors + rank
        low = ref[at : at + INDEX_ROWS].astype(F32)[:1].astype(jnp.int32)
        at += INDEX_ROWS
        high = ref[at : at + INDEX_ROWS].astype(F32)[:1].astype(jnp.int32)
        return ref[:vectors], ref[vectors : vectors + rank], high * 2**LOW_BITS + low

    base_own, step_own, rows_own = parts(block_ref)
    base_other, step_other, rows_other = parts(other_ref)
    base_even = jnp.where(odd, base_other, base_own)
    base_odd = jnp.where(odd, base_own, base_other)
    step_even = jnp.where(odd, step_other, step_own)
    step_odd = jnp.where(odd, step_own, step_other)
    pick_even = picker(jnp.where(odd, rows_other, rows_own), top_rows)
    pick_odd = picker(jnp.where(odd, rows_own, rows_other), top_rows)

    past = (dot(pick_even, step_even) - pick_odd.astype(F32)).astype(BF16)
    hop_fixed_ref[...] = base_odd.astype(F32) - dot(base_even, step_odd)
    hop_ref[...] = dot(past, step_odd).astype(BF16)
    for ref in hop_slope:
        ref[...] = dot(step_even, step_odd).astype(BF16)
    reach_ref[...] = jnp.where(odd, -past, pick_even)
    gain = gain_ref[...]
    fixed_ref[...] = base_ref[...] - dot(jnp.where(odd, base_even, jnp.zeros_like(base_even)), gain)
    slope_ref[...] = jnp.where(odd, -dot(step_even, gain), gain.astype(F32)).astype(BF16)


def last_kernel(level, own_ref, cross_ref, held_ref, swap_ref, top_ref):
    top_ref[...] = mixed(held_ref[...], swap_ref[...], own_ref[level], cross_ref[level]).astype(BF16)


def pass_kernel(hop_fixed_ref, hop_ref, *refs):
    *slabs, top_ref, pass_ref, wide = refs
    rows = slabs[0].shape[0]
    place = lax.axis_index("fr")
    for flip, slab in enumerate(slabs):
        start = pl.multiple_of(jnp.bitwise_xor(place, flip) * rows, rows)
        wide[pl.ds(start, rows), :] = slab[...].astype(F32)
    top = wide[...].astype(BF16)
    top_ref[...] = top
    pass_ref[...] = (hop_fixed_ref[...] + dot(top, hop_ref[...])).astype(BF16)


def link_kernel(fixed_ref, reach_ref, gain_ref, top_ref, out_ref):
    link = dot(top_ref[...], reach_ref[...]).astype(BF16)
    out_ref[...] = fixed_ref[...] - dot(link, gain_ref[...])


def final_kernel(fixed_ref, slope_ref, arrived_ref, top_ref, out_hbm, top_hbm, held, sems):
    first = pltpu.make_async_copy(top_ref, top_hbm, sems.at[0])
    first.start()
    arrived = jnp.where(lax.axis_index("fr") >= 2, arrived_ref[...].astype(F32), 0.0).astype(BF16)
    parts = sems.shape[0] - 1
    width = held.shape[1] // parts
    copies = [first]
    for part in range(parts):
        cut = pl.ds(part * width, width)
        held[:, cut] = (fixed_ref[:, cut] - dot(arrived, slope_ref[:, cut])).astype(BF16)
        copies.append(pltpu.make_async_copy(held.at[:, cut], out_hbm.at[:, cut], sems.at[part + 1]))
        copies[-1].start()
    for copy in copies:
        copy.wait()


def body(
    top_source,
    level_ordering,
    butterfly_own,
    butterfly_cross,
    parent_rows,
    front_source,
    panel_inverse,
    coupling_read,
    coupling_write,
):
    levels = level_ordering.shape[0]
    rows, top_rows = top_source.shape
    vectors, panel = front_source.shape
    rank = coupling_write.shape[0]
    groups, chain = lax.axis_size("bf"), lax.axis_size("fr")
    chips = chain // 2

    def flipped(array, mask):
        return lax.ppermute(array, "fr", [(i, i ^ mask) for i in range(chain)])

    def turned(array, by):
        return lax.ppermute(array, "fr", [(i, (i + by) % chain) for i in range(chain)])

    def swapped(array, mask):
        return lax.ppermute(array, "bf", [(g, g ^ mask) for g in range(groups)])

    held, order, own, cross = kernel_call(
        shuffle_kernel,
        [
            ((rows, top_rows), BF16, True),
            (level_ordering.shape, jnp.int32, True),
            (butterfly_own.shape, BF16, True),
            (butterfly_cross.shape, BF16, True),
        ],
        [pltpu.VMEM((rows, top_rows), BF16), pltpu.SemaphoreType.DMA((4,))],
        [],
        remote=[top_source, level_ordering, butterfly_own, butterfly_cross],
    )
    swap = swapped(held, 1)
    coupling_read, order = lax.optimization_barrier((coupling_read, order))
    next_read = turned(coupling_read, -1)
    (pick,) = kernel_call(
        pick_kernel, [((levels - 1, top_rows, top_rows), BF16, True)], [], [order]
    )

    panel_inverse, swap = lax.optimization_barrier((panel_inverse, swap))
    gain, base = kernel_call(
        panel_kernel,
        [((rank, panel), BF16, True), ((vectors, panel), F32, True)],
        [
            pltpu.VMEM((rank + vectors, panel), BF16),
            pltpu.VMEM((panel, panel), BF16),
            pltpu.SemaphoreType.DMA((2 + panel // rank,)),
        ],
        [],
        PANEL_COST,
        [coupling_write, panel_inverse, front_source],
    )

    for level in range(levels - 1):
        if level:
            swap, gain = lax.optimization_barrier((swap, gain))
        (held,) = kernel_call(
            functools.partial(level_kernel, level),
            [((rows, top_rows), BF16, True)],
            [],
            [pick, own, cross, held, swap],
            LEVEL_COST,
        )
        swap = swapped(held, 2 ** (level + 1))

    next_read, held = lax.optimization_barrier((next_read, held))
    (block,) = kernel_call(
        block_kernel,
        [((vectors + rank + 2 * INDEX_ROWS, rank), BF16, True)],
        [],
        [gain, base, next_read, parent_rows],
        2 * (vectors + rank) * panel * rank,
    )
    other = flipped(block, 1)
    outs = [
        ((vectors, panel), F32, True),
        ((top_rows, rank), BF16, True),
        ((rank, panel), BF16, True),
        ((vectors, rank), F32, True),
        ((top_rows, rank), BF16, True),
    ] + [((rank, rank), BF16, True)] * (chips > 2)
    fixed, reach, slope, hop_fixed, hop, *hop_slope = kernel_call(
        chain_kernel, outs, [], [gain, base, block, other], 2 * rank * rank * panel
    )

    (top,) = kernel_call(
        functools.partial(last_kernel, levels - 1),
        [((rows, top_rows), BF16, True)],
        [],
        [own, cross, held, swap],
        LEVEL_COST,
    )
    slabs = [top] + [flipped(top, mask) for mask in range(1, chain)]
    whole, passed = kernel_call(
        pass_kernel,
        [((vectors, top_rows), BF16, True), ((vectors, rank), BF16, True)],
        [pltpu.VMEM((vectors, top_rows), F32)],
        [hop_fixed, hop, *slabs],
    )
    start = passed
    for _ in range(chips - 2):
        here = jnp.where(lax.axis_index("fr") >= 2, turned(passed, 2), 0)
        passed = (start.astype(F32) + dot(here, hop_slope[0])).astype(BF16)
    arrived = turned(passed, 2)
    (ready,) = kernel_call(
        link_kernel, [((vectors, panel), F32, True)], [], [fixed, reach, gain, whole]
    )
    solved, top = kernel_call(
        final_kernel,
        [((vectors, panel), BF16, False), ((rows, top_rows), BF16, False)],
        [pltpu.VMEM((vectors, panel), BF16), pltpu.SemaphoreType.DMA((5,))],
        [ready, slope, arrived, top],
    )
    return (top, solved)


def solution(mesh):
    placed = (
        P("fr", "bf"),
        P(None, "bf", None),
        P(None, "bf", None),
        P(None, "bf", None),
        P(("bf", "fr"), None),
        P(None, ("bf", "fr")),
        P(("bf", "fr"), None),
        P(("bf", "fr"), None),
        P(("bf", "fr"), None),
    )
    return jax.shard_map(
        body,
        mesh=mesh,
        in_specs=placed,
        out_specs=(P("fr", "bf"), P(None, ("bf", "fr"))),
        check_vma=False,
    )
```

```python
import functools

import jax
import jax.numpy as jnp
from jax import lax
from jax.experimental import pallas as pl
from jax.experimental.pallas import tpu as pltpu
from jax.sharding import PartitionSpec as P

BF16 = jnp.bfloat16
F32 = jnp.float32
LOW_BITS = 8
INDEX_ROWS = 16
PANEL_COST = 10**9
LEVEL_COST = 4 * 10**9

def dot(left, right):
    return jnp.dot(left, right, preferred_element_type=F32)


def picker(columns, size):
    rows = lax.broadcasted_iota(jnp.int32, (size, columns.shape[1]), 0)
    return jnp.where(rows == columns, 1.0, 0.0).astype(BF16)


def kernel_call(kernel, outs, scratch, operands, flops=0, remote=(), aliases=None):
    vmem, hbm = pl.BlockSpec(memory_space=pltpu.VMEM), pl.BlockSpec(memory_space=pltpu.HBM)
    shapes = [
        pltpu.VMEM(shape, dtype) if inside else jax.ShapeDtypeStruct(shape, dtype)
        for shape, dtype, inside in outs
    ]
    placed = [pltpu.with_memory_space_constraint(x, pltpu.VMEM) for x in operands]
    return pl.pallas_call(
        kernel,
        out_shape=shapes,
        in_specs=[vmem] * len(placed) + [hbm] * len(remote),
        out_specs=[vmem if inside else hbm for _, _, inside in outs],
        scratch_shapes=scratch,
        compiler_params=pltpu.CompilerParams(vmem_limit_bytes=24 * 1024 * 1024),
        input_output_aliases=aliases or {},
        cost_estimate=pl.CostEstimate(flops=flops, bytes_accessed=0, transcendentals=0),
    )(*placed, *[pltpu.with_memory_space_constraint(x, pltpu.HBM) for x in remote])


def shuffle_kernel(source_hbm, order_hbm, out_ref, order_ref, source, sems):
    copies = [
        pltpu.make_async_copy(order_hbm, order_ref, sems.at[0]),
        pltpu.make_async_copy(source_hbm, source, sems.at[1]),
    ]
    for copy in copies:
        copy.start()
    copies[0].wait()
    pick = picker(order_ref[0], source.shape[1])
    copies[1].wait()
    out_ref[...] = dot(source[...], pick).astype(BF16)


def pick_kernel(order_ref, own_hbm, cross_hbm, pick_ref, own_ref, cross_ref, sems):
    copies = [
        pltpu.make_async_copy(own_hbm, own_ref, sems.at[0]),
        pltpu.make_async_copy(cross_hbm, cross_ref, sems.at[1]),
    ]
    for copy in copies:
        copy.start()
    for level in range(pick_ref.shape[0]):
        pick_ref[level] = picker(order_ref[level + 1], pick_ref.shape[1])
    for copy in copies:
        copy.wait()


def panel_kernel(write_hbm, inverse_hbm, source_hbm, gain_ref, base_ref, left, inverse, sems):
    rank, size = gain_ref.shape
    part = rank
    copies = [
        pltpu.make_async_copy(write_hbm, left.at[:rank], sems.at[0]),
        pltpu.make_async_copy(source_hbm, left.at[rank:], sems.at[1]),
    ]
    for start in range(0, size, part):
        block = (pl.ds(start, part), pl.ds(0, start + part))
        copies.append(
            pltpu.make_async_copy(inverse_hbm.at[block], inverse.at[block], sems.at[2 + start // part])
        )
    for copy in copies:
        copy.start()
    for copy in copies:
        copy.wait()
    for start in range(0, size, part):
        cut = slice(start, start + part)
        product = dot(left[:, start:], inverse[start:, cut])
        gain_ref[:, cut] = product[:rank].astype(BF16)
        base_ref[:, cut] = product[rank:]


def block_kernel(gain_ref, base_ref, read_ref, rows_ref, block_ref):
    vectors, rank = base_ref.shape[0], gain_ref.shape[0]
    read = read_ref[...]
    block_ref[:vectors] = dot(base_ref[...].astype(BF16), read).astype(BF16)
    block_ref[vectors : vectors + rank] = dot(gain_ref[...], read).astype(BF16)
    rows = rows_ref[...]
    low = jnp.bitwise_and(rows, 2**LOW_BITS - 1)
    high = lax.shift_right_logical(rows, jnp.full(rows.shape, LOW_BITS, jnp.int32))
    at = vectors + rank
    for part in (low, high):
        wide = jnp.broadcast_to(part.astype(F32), (INDEX_ROWS, rank))
        block_ref[at : at + INDEX_ROWS] = wide.astype(BF16)
        at += INDEX_ROWS


def mixed(own_part, partner_part, own, cross):
    size = own.shape[0]
    pieces = []
    for start in range(0, own_part.shape[1], size):
        cut = slice(start, start + size)
        pieces.append(dot(own_part[:, cut], own) + dot(partner_part[:, cut], cross))
    return jnp.concatenate(pieces, axis=1)


def level_kernel(level, pick_ref, own_ref, cross_ref, held_ref, swap_ref, out_ref):
    mix = mixed(held_ref[...], swap_ref[...], own_ref[level], cross_ref[level])
    out_ref[...] = dot(mix.astype(BF16), pick_ref[level]).astype(BF16)


def chain_kernel(
    gain_ref, base_ref, block_ref, other_ref, fixed_ref, reach_ref, slope_ref, hop_fixed_ref, hop_ref, *hop_slope
):
    vectors, rank = base_ref.shape[0], gain_ref.shape[0]
    top_rows = hop_ref.shape[0]
    odd = lax.rem(lax.axis_index("fr"), 2) == 1

    def parts(ref):
        at = vectors + rank
        low = ref[at : at + INDEX_ROWS].astype(F32)[:1].astype(jnp.int32)
        at += INDEX_ROWS
        high = ref[at : at + INDEX_ROWS].astype(F32)[:1].astype(jnp.int32)
        return ref[:vectors], ref[vectors : vectors + rank], high * 2**LOW_BITS + low

    base_own, step_own, rows_own = parts(block_ref)
    base_other, step_other, rows_other = parts(other_ref)
    base_even = jnp.where(odd, base_other, base_own)
    base_odd = jnp.where(odd, base_own, base_other)
    step_even = jnp.where(odd, step_other, step_own)
    step_odd = jnp.where(odd, step_own, step_other)
    pick_even = picker(jnp.where(odd, rows_other, rows_own), top_rows)
    pick_odd = picker(jnp.where(odd, rows_own, rows_other), top_rows)

    past = (dot(pick_even, step_even) - pick_odd.astype(F32)).astype(BF16)
    hop_fixed_ref[...] = base_odd.astype(F32) - dot(base_even, step_odd)
    hop_ref[...] = dot(past, step_odd).astype(BF16)
    for ref in hop_slope:
        ref[...] = dot(step_even, step_odd).astype(BF16)
    reach_ref[...] = jnp.where(odd, -past, pick_even)
    gain = gain_ref[...]
    fixed_ref[...] = base_ref[...] - dot(jnp.where(odd, base_even, jnp.zeros_like(base_even)), gain)
    slope_ref[...] = jnp.where(odd, -dot(step_even, gain), gain.astype(F32)).astype(BF16)


def last_kernel(level, own_ref, cross_ref, held_ref, swap_ref, top_ref):
    top_ref[...] = mixed(held_ref[...], swap_ref[...], own_ref[level], cross_ref[level]).astype(BF16)


def pass_kernel(hop_fixed_ref, hop_ref, *refs):
    *slabs, top_ref, pass_ref, wide = refs
    rows = slabs[0].shape[0]
    place = lax.axis_index("fr")
    for flip, slab in enumerate(reversed(slabs)):
        start = pl.multiple_of(jnp.bitwise_xor(place, flip) * rows, rows)
        wide[pl.ds(start, rows), :] = slab[...].astype(F32)
    top = wide[...].astype(BF16)
    top_ref[...] = top
    pass_ref[...] = (hop_fixed_ref[...] + dot(top, hop_ref[...])).astype(BF16)


def written(out_hbm, held, sems, part):
    parts = sems.shape[0]
    width = held.shape[1] // parts
    copies = []
    for index in range(parts):
        cut = pl.ds(index * width, width)
        held[:, cut] = part(cut).astype(BF16)
        copies.append(pltpu.make_async_copy(held.at[:, cut], out_hbm.at[:, cut], sems.at[index]))
        copies[-1].start()
    for copy in copies:
        copy.wait()


def link_kernel(fixed_ref, reach_ref, gain_ref, whole_ref, top_ref, ready_ref, out_hbm, top_hbm, held, sems, top_sem):
    copy = pltpu.make_async_copy(top_ref, top_hbm, top_sem)
    copy.start()
    link = dot(whole_ref[...], reach_ref[...]).astype(BF16)
    ready_ref[...] = fixed_ref[...] - dot(link, gain_ref[...])

    @pl.when(lax.axis_index("fr") < 2)
    def _():
        written(out_hbm, held, sems, lambda cut: ready_ref[:, cut])

    copy.wait()


def final_kernel(ready_ref, slope_ref, arrived_ref, solved_hbm, out_hbm, held, sems):
    @pl.when(lax.axis_index("fr") >= 2)
    def _():
        arrived = arrived_ref[...]
        written(out_hbm, held, sems, lambda cut: ready_ref[:, cut] - dot(arrived, slope_ref[:, cut]))


def body(
    top_source,
    level_ordering,
    butterfly_own,
    butterfly_cross,
    parent_rows,
    front_source,
    panel_inverse,
    coupling_read,
    coupling_write,
):
    levels = level_ordering.shape[0]
    rows, top_rows = top_source.shape
    vectors, panel = front_source.shape
    rank = coupling_write.shape[0]
    groups, chain = lax.axis_size("bf"), lax.axis_size("fr")
    chips = chain // 2

    def flipped(array, mask):
        return lax.ppermute(array, "fr", [(i, i ^ mask) for i in range(chain)])

    def turned(array, by):
        return lax.ppermute(array, "fr", [(i, (i + by) % chain) for i in range(chain)])

    def swapped(array, mask):
        return lax.ppermute(array, "bf", [(g, g ^ mask) for g in range(groups)])

    held, order = kernel_call(
        shuffle_kernel,
        [((rows, top_rows), BF16, True), (level_ordering.shape, jnp.int32, True)],
        [pltpu.VMEM((rows, top_rows), BF16), pltpu.SemaphoreType.DMA((2,))],
        [],
        remote=[top_source, level_ordering],
    )
    swap = swapped(held, 1)
    coupling_read, order = lax.optimization_barrier((coupling_read, order))
    next_read = turned(coupling_read, -1)
    pick, own, cross = kernel_call(
        pick_kernel,
        [
            ((levels - 1, top_rows, top_rows), BF16, True),
            (butterfly_own.shape, BF16, True),
            (butterfly_cross.shape, BF16, True),
        ],
        [pltpu.SemaphoreType.DMA((2,))],
        [order],
        remote=[butterfly_own, butterfly_cross],
    )

    panel_inverse, swap = lax.optimization_barrier((panel_inverse, swap))
    gain, base = kernel_call(
        panel_kernel,
        [((rank, panel), BF16, True), ((vectors, panel), F32, True)],
        [
            pltpu.VMEM((rank + vectors, panel), BF16),
            pltpu.VMEM((panel, panel), BF16),
            pltpu.SemaphoreType.DMA((2 + panel // rank,)),
        ],
        [],
        PANEL_COST,
        [coupling_write, panel_inverse, front_source],
    )

    for level in range(levels - 1):
        if level:
            swap, gain = lax.optimization_barrier((swap, gain))
        (held,) = kernel_call(
            functools.partial(level_kernel, level),
            [((rows, top_rows), BF16, True)],
            [],
            [pick, own, cross, held, swap],
            LEVEL_COST,
        )
        swap = swapped(held, 2 ** (level + 1))

    next_read, held = lax.optimization_barrier((next_read, held))
    (block,) = kernel_call(
        block_kernel,
        [((vectors + rank + 2 * INDEX_ROWS, rank), BF16, True)],
        [],
        [gain, base, next_read, parent_rows],
        2 * (vectors + rank) * panel * rank,
    )
    other = flipped(block, 1)
    outs = [
        ((vectors, panel), F32, True),
        ((top_rows, rank), BF16, True),
        ((rank, panel), BF16, True),
        ((vectors, rank), F32, True),
        ((top_rows, rank), BF16, True),
    ] + [((rank, rank), BF16, True)] * (chips > 2)
    fixed, reach, slope, hop_fixed, hop, *hop_slope = kernel_call(
        chain_kernel, outs, [], [gain, base, block, other], 2 * rank * rank * panel
    )

    (top,) = kernel_call(
        functools.partial(last_kernel, levels - 1),
        [((rows, top_rows), BF16, True)],
        [],
        [own, cross, held, swap],
        LEVEL_COST,
    )
    slabs = [flipped(top, mask) for mask in range(chain - 1, 0, -1)] + [top]
    whole, passed = kernel_call(
        pass_kernel,
        [((vectors, top_rows), BF16, True), ((vectors, rank), BF16, True)],
        [pltpu.VMEM((vectors, top_rows), F32)],
        [hop_fixed, hop, *slabs],
    )
    start = passed
    for _ in range(chips - 2):
        here = jnp.where(lax.axis_index("fr") >= 2, turned(passed, 2), 0)
        passed = (start.astype(F32) + dot(here, hop_slope[0])).astype(BF16)
    arrived = turned(passed, 2)
    staging = [pltpu.VMEM((vectors, panel), BF16), pltpu.SemaphoreType.DMA((4,))]
    ready, solved, top = kernel_call(
        link_kernel,
        [((vectors, panel), F32, True), ((vectors, panel), BF16, False), ((rows, top_rows), BF16, False)],
        [*staging, pltpu.SemaphoreType.DMA],
        [fixed, reach, gain, whole, top],
    )
    (solved,) = kernel_call(
        final_kernel,
        [((vectors, panel), BF16, False)],
        staging,
        [ready, slope, arrived],
        remote=[solved],
        aliases={3: 0},
    )
    return (top, solved)


def solution(mesh):
    placed = (
        P("fr", "bf"),
        P(None, "bf", None),
        P(None, "bf", None),
        P(None, "bf", None),
        P(("bf", "fr"), None),
        P(None, ("bf", "fr")),
        P(("bf", "fr"), None),
        P(("bf", "fr"), None),
        P(("bf", "fr"), None),
    )
    return jax.shard_map(
        body,
        mesh=mesh,
        in_specs=placed,
        out_specs=(P("fr", "bf"), P(None, ("bf", "fr"))),
        check_vma=False,
    )
```

```python
import functools

import jax
import jax.numpy as jnp
from jax import lax
from jax.experimental import pallas as pl
from jax.experimental.pallas import tpu as pltpu
from jax.sharding import PartitionSpec as P

BF16 = jnp.bfloat16
F32 = jnp.float32
LOW_BITS = 8
INDEX_ROWS = 16
PANEL_COST = 10**9
LEVEL_COST = 4 * 10**9

def dot(left, right):
    return jnp.dot(left, right, preferred_element_type=F32)


def picker(columns, size):
    rows = lax.broadcasted_iota(jnp.int32, (size, columns.shape[1]), 0)
    return jnp.where(rows == columns, 1.0, 0.0).astype(BF16)


def kernel_call(kernel, outs, scratch, operands, flops=0, remote=(), aliases=None):
    vmem, hbm = pl.BlockSpec(memory_space=pltpu.VMEM), pl.BlockSpec(memory_space=pltpu.HBM)
    shapes = [
        pltpu.VMEM(shape, dtype) if inside else jax.ShapeDtypeStruct(shape, dtype)
        for shape, dtype, inside in outs
    ]
    placed = [pltpu.with_memory_space_constraint(x, pltpu.VMEM) for x in operands]
    return pl.pallas_call(
        kernel,
        out_shape=shapes,
        in_specs=[vmem] * len(placed) + [hbm] * len(remote),
        out_specs=[vmem if inside else hbm for _, _, inside in outs],
        scratch_shapes=scratch,
        compiler_params=pltpu.CompilerParams(vmem_limit_bytes=24 * 1024 * 1024),
        input_output_aliases=aliases or {},
        cost_estimate=pl.CostEstimate(flops=flops, bytes_accessed=0, transcendentals=0),
    )(*placed, *[pltpu.with_memory_space_constraint(x, pltpu.HBM) for x in remote])


def shuffle_kernel(source_hbm, order_hbm, out_ref, order_ref, source, sems):
    copies = [
        pltpu.make_async_copy(order_hbm, order_ref, sems.at[0]),
        pltpu.make_async_copy(source_hbm, source, sems.at[1]),
    ]
    for copy in copies:
        copy.start()
    copies[0].wait()
    pick = picker(order_ref[0], source.shape[1])
    copies[1].wait()
    out_ref[...] = dot(source[...], pick).astype(BF16)


def fold(factor, pick):
    size = factor.shape[0]
    pieces = [dot(factor, pick[start : start + size]) for start in range(0, pick.shape[0], size)]
    return jnp.concatenate(pieces, axis=0).astype(BF16)


def ready_kernel(order_ref, held_ref, own_hbm, cross_hbm, part_ref, fold_ref, own_ref, cross_ref, sems):
    copies = [
        pltpu.make_async_copy(own_hbm, own_ref, sems.at[0]),
        pltpu.make_async_copy(cross_hbm, cross_ref, sems.at[1]),
    ]
    for copy in copies:
        copy.start()
    pick = picker(order_ref[1], held_ref.shape[1])
    for copy in copies:
        copy.wait()
    part_ref[...] = dot(held_ref[...], fold(own_ref[0], pick))
    fold_ref[...] = fold(cross_ref[0], pick)


def panel_kernel(
    level, order_ref, held_ref, own_ref, cross_ref, write_hbm, inverse_hbm, source_hbm,
    part_ref, fold_ref, gain_ref, base_ref, left, inverse, sems,
):
    rank, size = gain_ref.shape
    part = rank
    copies = [
        pltpu.make_async_copy(write_hbm, left.at[:rank], sems.at[0]),
        pltpu.make_async_copy(source_hbm, left.at[rank:], sems.at[1]),
    ]
    for start in range(0, size, part):
        block = (pl.ds(start, part), pl.ds(0, start + part))
        copies.append(
            pltpu.make_async_copy(inverse_hbm.at[block], inverse.at[block], sems.at[2 + start // part])
        )
    for copy in copies:
        copy.start()
    pick = picker(order_ref[level + 1], held_ref.shape[1])
    part_ref[...] = dot(held_ref[...], fold(own_ref[level], pick))
    fold_ref[...] = fold(cross_ref[level], pick)
    for copy in copies:
        copy.wait()
    for start in range(0, size, part):
        cut = slice(start, start + part)
        product = dot(left[:, start:], inverse[start:, cut])
        gain_ref[:, cut] = product[:rank].astype(BF16)
        base_ref[:, cut] = product[rank:]


def block_kernel(gain_ref, base_ref, read_ref, rows_ref, block_ref):
    vectors, rank = base_ref.shape[0], gain_ref.shape[0]
    read = read_ref[...]
    block_ref[:vectors] = dot(base_ref[...].astype(BF16), read).astype(BF16)
    block_ref[vectors : vectors + rank] = dot(gain_ref[...], read).astype(BF16)
    rows = rows_ref[...]
    low = jnp.bitwise_and(rows, 2**LOW_BITS - 1)
    high = lax.shift_right_logical(rows, jnp.full(rows.shape, LOW_BITS, jnp.int32))
    at = vectors + rank
    for part in (low, high):
        wide = jnp.broadcast_to(part.astype(F32), (INDEX_ROWS, rank))
        block_ref[at : at + INDEX_ROWS] = wide.astype(BF16)
        at += INDEX_ROWS


def mixed(own_part, partner_part, own, cross):
    size = own.shape[0]
    pieces = []
    for start in range(0, own_part.shape[1], size):
        cut = slice(start, start + size)
        pieces.append(dot(own_part[:, cut], own) + dot(partner_part[:, cut], cross))
    return jnp.concatenate(pieces, axis=1)


def level_kernel(part_ref, fold_ref, swap_ref, out_ref):
    out_ref[...] = (part_ref[...] + dot(swap_ref[...], fold_ref[...])).astype(BF16)


def chain_kernel(
    gain_ref, base_ref, block_ref, other_ref, fixed_ref, reach_ref, slope_ref, hop_fixed_ref, hop_ref, *hop_slope
):
    vectors, rank = base_ref.shape[0], gain_ref.shape[0]
    top_rows = hop_ref.shape[0]
    odd = lax.rem(lax.axis_index("fr"), 2) == 1

    def parts(ref):
        at = vectors + rank
        low = ref[at : at + INDEX_ROWS].astype(F32)[:1].astype(jnp.int32)
        at += INDEX_ROWS
        high = ref[at : at + INDEX_ROWS].astype(F32)[:1].astype(jnp.int32)
        return ref[:vectors], ref[vectors : vectors + rank], high * 2**LOW_BITS + low

    base_own, step_own, rows_own = parts(block_ref)
    base_other, step_other, rows_other = parts(other_ref)
    base_even = jnp.where(odd, base_other, base_own)
    base_odd = jnp.where(odd, base_own, base_other)
    step_even = jnp.where(odd, step_other, step_own)
    step_odd = jnp.where(odd, step_own, step_other)
    pick_even = picker(jnp.where(odd, rows_other, rows_own), top_rows)
    pick_odd = picker(jnp.where(odd, rows_own, rows_other), top_rows)

    past = (dot(pick_even, step_even) - pick_odd.astype(F32)).astype(BF16)
    hop_fixed_ref[...] = base_odd.astype(F32) - dot(base_even, step_odd)
    hop_ref[...] = dot(past, step_odd).astype(BF16)
    for ref in hop_slope:
        ref[...] = dot(step_even, step_odd).astype(BF16)
    reach_ref[...] = jnp.where(odd, -past, pick_even)
    gain = gain_ref[...]
    fixed_ref[...] = base_ref[...] - dot(jnp.where(odd, base_even, jnp.zeros_like(base_even)), gain)
    slope_ref[...] = jnp.where(odd, -dot(step_even, gain), gain.astype(F32)).astype(BF16)


def last_kernel(level, own_ref, cross_ref, held_ref, swap_ref, top_ref):
    top_ref[...] = mixed(held_ref[...], swap_ref[...], own_ref[level], cross_ref[level]).astype(BF16)


def pass_kernel(hop_fixed_ref, hop_ref, *refs):
    *slabs, top_ref, pass_ref, wide = refs
    rows = slabs[0].shape[0]
    place = lax.axis_index("fr")
    for flip, slab in enumerate(slabs):
        start = pl.multiple_of(jnp.bitwise_xor(place, flip) * rows, rows)
        wide[pl.ds(start, rows), :] = slab[...].astype(F32)
    top = wide[...].astype(BF16)
    top_ref[...] = top
    pass_ref[...] = (hop_fixed_ref[...] + dot(top, hop_ref[...])).astype(BF16)


def written(out_hbm, held, sems, part):
    parts = sems.shape[0]
    width = held.shape[1] // parts
    copies = []
    for index in range(parts):
        cut = pl.ds(index * width, width)
        held[:, cut] = part(cut).astype(BF16)
        copies.append(pltpu.make_async_copy(held.at[:, cut], out_hbm.at[:, cut], sems.at[index]))
        copies[-1].start()
    for copy in copies:
        copy.wait()


def link_kernel(fixed_ref, reach_ref, gain_ref, whole_ref, top_ref, ready_ref, out_hbm, top_hbm, held, sems, top_sem):
    copy = pltpu.make_async_copy(top_ref, top_hbm, top_sem)
    copy.start()
    link = dot(whole_ref[...], reach_ref[...]).astype(BF16)
    ready_ref[...] = fixed_ref[...] - dot(link, gain_ref[...])

    @pl.when(lax.axis_index("fr") < 2)
    def _():
        written(out_hbm, held, sems, lambda cut: ready_ref[:, cut])

    copy.wait()


def final_kernel(ready_ref, slope_ref, arrived_ref, solved_hbm, out_hbm, held, sems):
    @pl.when(lax.axis_index("fr") >= 2)
    def _():
        arrived = arrived_ref[...]
        written(out_hbm, held, sems, lambda cut: ready_ref[:, cut] - dot(arrived, slope_ref[:, cut]))


def body(
    top_source,
    level_ordering,
    butterfly_own,
    butterfly_cross,
    parent_rows,
    front_source,
    panel_inverse,
    coupling_read,
    coupling_write,
):
    levels = level_ordering.shape[0]
    rows, top_rows = top_source.shape
    vectors, panel = front_source.shape
    rank = coupling_write.shape[0]
    groups, chain = lax.axis_size("bf"), lax.axis_size("fr")
    chips = chain // 2

    def flipped(array, mask):
        return lax.ppermute(array, "fr", [(i, i ^ mask) for i in range(chain)])

    def turned(array, by):
        return lax.ppermute(array, "fr", [(i, (i + by) % chain) for i in range(chain)])

    def swapped(array, mask):
        return lax.ppermute(array, "bf", [(g, g ^ mask) for g in range(groups)])

    held, order = kernel_call(
        shuffle_kernel,
        [((rows, top_rows), BF16, True), (level_ordering.shape, jnp.int32, True)],
        [pltpu.VMEM((rows, top_rows), BF16), pltpu.SemaphoreType.DMA((2,))],
        [],
        remote=[top_source, level_ordering],
    )
    swap = swapped(held, 1)
    coupling_read, order = lax.optimization_barrier((coupling_read, order))
    next_read = turned(coupling_read, -1)
    ready_outs = [((rows, top_rows), F32, True), ((top_rows, top_rows), BF16, True)]
    part, folded, own, cross = kernel_call(
        ready_kernel,
        [*ready_outs, (butterfly_own.shape, BF16, True), (butterfly_cross.shape, BF16, True)],
        [pltpu.SemaphoreType.DMA((2,))],
        [order, held],
        remote=[butterfly_own, butterfly_cross],
    )

    def next_level(part, folded, swap):
        return kernel_call(
            level_kernel, [((rows, top_rows), BF16, True)], [], [part, folded, swap], LEVEL_COST
        )[0]

    held = next_level(part, folded, swap)
    swap = swapped(held, 2)
    part, folded, gain, base = kernel_call(
        functools.partial(panel_kernel, 1),
        [*ready_outs, ((rank, panel), BF16, True), ((vectors, panel), F32, True)],
        [
            pltpu.VMEM((rank + vectors, panel), BF16),
            pltpu.VMEM((panel, panel), BF16),
            pltpu.SemaphoreType.DMA((2 + panel // rank,)),
        ],
        [order, held, own, cross],
        PANEL_COST,
        [coupling_write, panel_inverse, front_source],
    )
    held = next_level(part, folded, swap)
    swap = swapped(held, 4)

    next_read, held = lax.optimization_barrier((next_read, held))
    (block,) = kernel_call(
        block_kernel,
        [((vectors + rank + 2 * INDEX_ROWS, rank), BF16, True)],
        [],
        [gain, base, next_read, parent_rows],
        2 * (vectors + rank) * panel * rank,
    )
    other = flipped(block, 1)
    outs = [
        ((vectors, panel), F32, True),
        ((top_rows, rank), BF16, True),
        ((rank, panel), BF16, True),
        ((vectors, rank), F32, True),
        ((top_rows, rank), BF16, True),
    ] + [((rank, rank), BF16, True)] * (chips > 2)
    fixed, reach, slope, hop_fixed, hop, *hop_slope = kernel_call(
        chain_kernel, outs, [], [gain, base, block, other], 2 * rank * rank * panel
    )

    (top,) = kernel_call(
        functools.partial(last_kernel, levels - 1),
        [((rows, top_rows), BF16, True)],
        [],
        [own, cross, held, swap],
        LEVEL_COST,
    )
    slabs = [top] + [flipped(top, mask) for mask in range(1, chain)]
    whole, passed = kernel_call(
        pass_kernel,
        [((vectors, top_rows), BF16, True), ((vectors, rank), BF16, True)],
        [pltpu.VMEM((vectors, top_rows), F32)],
        [hop_fixed, hop, *slabs],
    )
    start = passed
    for _ in range(chips - 2):
        here = jnp.where(lax.axis_index("fr") >= 2, turned(passed, 2), 0)
        passed = (start.astype(F32) + dot(here, hop_slope[0])).astype(BF16)
    arrived = turned(passed, 2)
    staging = [pltpu.VMEM((vectors, panel), BF16), pltpu.SemaphoreType.DMA((4,))]
    ready, solved, top = kernel_call(
        link_kernel,
        [((vectors, panel), F32, True), ((vectors, panel), BF16, False), ((rows, top_rows), BF16, False)],
        [*staging, pltpu.SemaphoreType.DMA],
        [fixed, reach, gain, whole, top],
    )
    (solved,) = kernel_call(
        final_kernel,
        [((vectors, panel), BF16, False)],
        staging,
        [ready, slope, arrived],
        remote=[solved],
        aliases={3: 0},
    )
    return (top, solved)


def solution(mesh):
    placed = (
        P("fr", "bf"),
        P(None, "bf", None),
        P(None, "bf", None),
        P(None, "bf", None),
        P(("bf", "fr"), None),
        P(None, ("bf", "fr")),
        P(("bf", "fr"), None),
        P(("bf", "fr"), None),
        P(("bf", "fr"), None),
    )
    return jax.shard_map(
        body,
        mesh=mesh,
        in_specs=placed,
        out_specs=(P("fr", "bf"), P(None, ("bf", "fr"))),
        check_vma=False,
    )
```

```python
import functools

import jax
import jax.numpy as jnp
from jax import lax
from jax.experimental import pallas as pl
from jax.experimental.pallas import tpu as pltpu
from jax.sharding import PartitionSpec as P

BF16 = jnp.bfloat16
F32 = jnp.float32
LOW_BITS = 8
INDEX_ROWS = 16
PANEL_COST = 10**9
CHAIN_COST = 3 * 10**9
PRIOR_COST = 10**9
LAST_COST = 10**8
LEVEL_COST = 2 * 10**9

def dot(left, right):
    return jnp.dot(left, right, preferred_element_type=F32)


def picker(columns, size):
    rows = lax.broadcasted_iota(jnp.int32, (size, columns.shape[1]), 0)
    return jnp.where(rows == columns, 1.0, 0.0).astype(BF16)


def kernel_call(kernel, outs, scratch, operands, flops=0, remote=(), aliases=None):
    vmem, hbm = pl.BlockSpec(memory_space=pltpu.VMEM), pl.BlockSpec(memory_space=pltpu.HBM)
    shapes = [
        pltpu.VMEM(shape, dtype) if inside else jax.ShapeDtypeStruct(shape, dtype)
        for shape, dtype, inside in outs
    ]
    placed = [pltpu.with_memory_space_constraint(x, pltpu.VMEM) for x in operands]
    return pl.pallas_call(
        kernel,
        out_shape=shapes,
        in_specs=[vmem] * len(placed) + [hbm] * len(remote),
        out_specs=[vmem if inside else hbm for _, _, inside in outs],
        scratch_shapes=scratch,
        compiler_params=pltpu.CompilerParams(vmem_limit_bytes=24 * 1024 * 1024),
        input_output_aliases=aliases or {},
        cost_estimate=pl.CostEstimate(flops=flops, bytes_accessed=0, transcendentals=0),
    )(*placed, *[pltpu.with_memory_space_constraint(x, pltpu.HBM) for x in remote])


def shuffle_kernel(source_hbm, order_hbm, out_ref, order_ref, source, sems):
    copies = [
        pltpu.make_async_copy(order_hbm, order_ref, sems.at[0]),
        pltpu.make_async_copy(source_hbm, source, sems.at[1]),
    ]
    for copy in copies:
        copy.start()
    copies[0].wait()
    pick = picker(order_ref[0], source.shape[1])
    copies[1].wait()
    out_ref[...] = dot(source[...], pick).astype(BF16)


def fold(factor, pick):
    size = factor.shape[0]
    pieces = [dot(factor, pick[start : start + size]) for start in range(0, pick.shape[0], size)]
    return jnp.concatenate(pieces, axis=0).astype(BF16)


def ready_kernel(
    order_ref, held_ref, own_hbm, cross_hbm, rows_hbm, part_ref, fold_ref, own_ref, cross_ref, rows_ref, sems
):
    copies = [
        pltpu.make_async_copy(own_hbm, own_ref, sems.at[0]),
        pltpu.make_async_copy(cross_hbm, cross_ref, sems.at[1]),
        pltpu.make_async_copy(rows_hbm, rows_ref, sems.at[2]),
    ]
    for copy in copies:
        copy.start()
    pick = picker(order_ref[1], held_ref.shape[1])
    for copy in copies:
        copy.wait()
    part_ref[...] = dot(held_ref[...], fold(own_ref[0], pick))
    fold_ref[...] = fold(cross_ref[0], pick)


def panel_kernel(
    level, order_ref, held_ref, own_ref, cross_ref, write_hbm, inverse_hbm, source_hbm,
    part_ref, fold_ref, gain_ref, base_ref, left, inverse, sems,
):
    rank, size = gain_ref.shape
    part = rank
    copies = [
        pltpu.make_async_copy(write_hbm, left.at[:rank], sems.at[0]),
        pltpu.make_async_copy(source_hbm, left.at[rank:], sems.at[1]),
    ]
    for start in range(0, size, part):
        block = (pl.ds(start, part), pl.ds(0, start + part))
        copies.append(
            pltpu.make_async_copy(inverse_hbm.at[block], inverse.at[block], sems.at[2 + start // part])
        )
    for copy in copies:
        copy.start()
    pick = picker(order_ref[level + 1], held_ref.shape[1])
    part_ref[...] = dot(held_ref[...], fold(own_ref[level], pick))
    fold_ref[...] = fold(cross_ref[level], pick)
    for copy in copies:
        copy.wait()
    for start in range(0, size, part):
        cut = slice(start, start + part)
        product = dot(left[:, start:], inverse[start:, cut])
        gain_ref[:, cut] = product[:rank].astype(BF16)
        base_ref[:, cut] = product[rank:]


def block_kernel(gain_ref, base_ref, read_ref, rows_ref, block_ref):
    vectors, rank = base_ref.shape[0], gain_ref.shape[0]
    read = read_ref[...]
    block_ref[:vectors] = dot(base_ref[...].astype(BF16), read).astype(BF16)
    block_ref[vectors : vectors + rank] = dot(gain_ref[...], read).astype(BF16)
    rows = rows_ref[...]
    low = jnp.bitwise_and(rows, 2**LOW_BITS - 1)
    high = lax.shift_right_logical(rows, jnp.full(rows.shape, LOW_BITS, jnp.int32))
    at = vectors + rank
    for part in (low, high):
        wide = jnp.broadcast_to(part.astype(F32), (INDEX_ROWS, rank))
        block_ref[at : at + INDEX_ROWS] = wide.astype(BF16)
        at += INDEX_ROWS


def mixed(own_part, partner_part, own, cross):
    size = own.shape[0]
    pieces = []
    for start in range(0, own_part.shape[1], size):
        cut = slice(start, start + size)
        pieces.append(dot(own_part[:, cut], own) + dot(partner_part[:, cut], cross))
    return jnp.concatenate(pieces, axis=1)


def level_kernel(part_ref, fold_ref, swap_ref, out_ref):
    out_ref[...] = (part_ref[...] + dot(swap_ref[...], fold_ref[...])).astype(BF16)


def pair_blocks(own_ref, other_ref, vectors, rank, top_rows):
    odd = lax.rem(lax.axis_index("fr"), 2) == 1

    def parts(ref):
        at = vectors + rank
        low = ref[at : at + INDEX_ROWS].astype(F32)[:1].astype(jnp.int32)
        at += INDEX_ROWS
        high = ref[at : at + INDEX_ROWS].astype(F32)[:1].astype(jnp.int32)
        return ref[:vectors], ref[vectors : vectors + rank], high * 2**LOW_BITS + low

    own, other = parts(own_ref), parts(other_ref)
    base_even, step_even, rows_even = (jnp.where(odd, y, x) for x, y in zip(own, other))
    base_odd, step_odd, rows_odd = (jnp.where(odd, x, y) for x, y in zip(own, other))
    pick_even, pick_odd = picker(rows_even, top_rows), picker(rows_odd, top_rows)
    past = (dot(pick_even, step_even) - pick_odd.astype(F32)).astype(BF16)
    return odd, base_even, base_odd, step_even, step_odd, pick_even, past


def chain_kernel(gain_ref, base_ref, block_ref, other_ref, fixed_ref, reach_ref, slope_ref, *hops):
    vectors, rank, top_rows = base_ref.shape[0], gain_ref.shape[0], reach_ref.shape[0]
    odd, base_even, base_odd, step_even, step_odd, pick_even, past = pair_blocks(
        block_ref, other_ref, vectors, rank, top_rows
    )
    if hops:
        hop_fixed_ref, hop_ref, hop_slope_ref = hops
        hop_fixed_ref[...] = base_odd.astype(F32) - dot(base_even, step_odd)
        hop_ref[...] = dot(past, step_odd).astype(BF16)
        hop_slope_ref[...] = dot(step_even, step_odd).astype(BF16)
    reach_ref[...] = jnp.where(odd, -past, pick_even)
    gain = gain_ref[...]
    fixed_ref[...] = base_ref[...] - dot(jnp.where(odd, base_even, jnp.zeros_like(base_even)), gain)
    slope_ref[...] = jnp.where(odd, -dot(step_even, gain), gain.astype(F32)).astype(BF16)


def prior_kernel(block_ref, other_ref, fixed_ref, reach_ref):
    (vectors, rank), top_rows = fixed_ref.shape, reach_ref.shape[0]
    _, base_even, base_odd, _, step_odd, _, past = pair_blocks(
        block_ref, other_ref, vectors, rank, top_rows
    )
    later = lax.axis_index("fr") >= 2
    fixed_ref[...] = jnp.where(later, base_odd.astype(F32) - dot(base_even, step_odd), 0.0)
    reach_ref[...] = jnp.where(later, dot(past, step_odd), 0.0).astype(BF16)


def last_kernel(level, own_ref, cross_ref, held_ref, swap_ref, top_ref):
    top_ref[...] = mixed(held_ref[...], swap_ref[...], own_ref[level], cross_ref[level]).astype(BF16)


def gathered(wide, slabs):
    rows = slabs[0].shape[0]
    place = lax.axis_index("fr")
    for flip, slab in enumerate(slabs):
        start = pl.multiple_of(jnp.bitwise_xor(place, flip) * rows, rows)
        wide[pl.ds(start, rows), :] = slab[...].astype(F32)
    return wide[...].astype(BF16)


def pass_kernel(hop_fixed_ref, hop_ref, *refs):
    *slabs, top_ref, pass_ref, wide = refs
    top = gathered(wide, slabs)
    top_ref[...] = top
    pass_ref[...] = (hop_fixed_ref[...] + dot(top, hop_ref[...])).astype(BF16)


def written(out_hbm, held, sems, part):
    parts = sems.shape[0]
    width = held.shape[1] // parts
    copies = []
    for index in range(parts):
        cut = pl.ds(index * width, width)
        held[:, cut] = part(cut).astype(BF16)
        copies.append(pltpu.make_async_copy(held.at[:, cut], out_hbm.at[:, cut], sems.at[index]))
        copies[-1].start()
    for copy in copies:
        copy.wait()


def link_kernel(fixed_ref, reach_ref, gain_ref, whole_ref, top_ref, ready_ref, out_hbm, top_hbm, held, sems, top_sem):
    copy = pltpu.make_async_copy(top_ref, top_hbm, top_sem)
    copy.start()
    link = dot(whole_ref[...], reach_ref[...]).astype(BF16)
    ready_ref[...] = fixed_ref[...] - dot(link, gain_ref[...])

    @pl.when(lax.axis_index("fr") < 2)
    def _():
        written(out_hbm, held, sems, lambda cut: ready_ref[:, cut])

    copy.wait()


def final_kernel(ready_ref, slope_ref, arrived_ref, solved_hbm, out_hbm, held, sems):
    @pl.when(lax.axis_index("fr") >= 2)
    def _():
        arrived = arrived_ref[...]
        written(out_hbm, held, sems, lambda cut: ready_ref[:, cut] - dot(arrived, slope_ref[:, cut]))


def whole_kernel(fixed_ref, reach_ref, gain_ref, slope_ref, prior_fixed_ref, prior_ref, *refs):
    *slabs, out_hbm, top_hbm, wide, held, sems, top_sem = refs
    copy = pltpu.make_async_copy(slabs[0], top_hbm, top_sem)
    copy.start()
    top = gathered(wide, slabs)
    link = dot(top, reach_ref[...]).astype(BF16)
    prior = (prior_fixed_ref[...] + dot(top, prior_ref[...])).astype(BF16)

    def part(cut):
        return fixed_ref[:, cut] - (dot(link, gain_ref[:, cut]) + dot(prior, slope_ref[:, cut]))

    written(out_hbm, held, sems, part)
    copy.wait()


def body(
    top_source,
    level_ordering,
    butterfly_own,
    butterfly_cross,
    parent_rows,
    front_source,
    panel_inverse,
    coupling_read,
    coupling_write,
):
    levels = level_ordering.shape[0]
    rows, top_rows = top_source.shape
    vectors, panel = front_source.shape
    rank = coupling_write.shape[0]
    groups, chain = lax.axis_size("bf"), lax.axis_size("fr")
    chips = chain // 2

    def flipped(array, mask):
        return lax.ppermute(array, "fr", [(i, i ^ mask) for i in range(chain)])

    def turned(array, by):
        return lax.ppermute(array, "fr", [(i, (i + by) % chain) for i in range(chain)])

    def swapped(array, mask):
        return lax.ppermute(array, "bf", [(g, g ^ mask) for g in range(groups)])

    held, order = kernel_call(
        shuffle_kernel,
        [((rows, top_rows), BF16, True), (level_ordering.shape, jnp.int32, True)],
        [pltpu.VMEM((rows, top_rows), BF16), pltpu.SemaphoreType.DMA((2,))],
        [],
        remote=[top_source, level_ordering],
    )
    swap = swapped(held, 1)
    if chips > 2:
        coupling_read, order = lax.optimization_barrier((coupling_read, order))
    next_read = turned(coupling_read, -1)
    ready_outs = [((rows, top_rows), F32, True), ((top_rows, top_rows), BF16, True)]
    part, folded, own, cross, parent_rows = kernel_call(
        ready_kernel,
        [
            *ready_outs,
            (butterfly_own.shape, BF16, True),
            (butterfly_cross.shape, BF16, True),
            (parent_rows.shape, jnp.int32, True),
        ],
        [pltpu.SemaphoreType.DMA((3,))],
        [order, held],
        remote=[butterfly_own, butterfly_cross, parent_rows],
    )

    def next_level(part, folded, swap):
        return kernel_call(
            level_kernel, [((rows, top_rows), BF16, True)], [], [part, folded, swap], LEVEL_COST
        )[0]

    held = next_level(part, folded, swap)
    swap = swapped(held, 2)
    part, folded, gain, base = kernel_call(
        functools.partial(panel_kernel, 1),
        [*ready_outs, ((rank, panel), BF16, True), ((vectors, panel), F32, True)],
        [
            pltpu.VMEM((rank + vectors, panel), BF16),
            pltpu.VMEM((panel, panel), BF16),
            pltpu.SemaphoreType.DMA((2 + panel // rank,)),
        ],
        [order, held, own, cross],
        PANEL_COST,
        [coupling_write, panel_inverse, front_source],
    )
    held = next_level(part, folded, swap)

    if chips > 2:
        swap = swapped(held, 4)
    next_read, held = lax.optimization_barrier((next_read, held))
    (block,) = kernel_call(
        block_kernel,
        [((vectors + rank + 2 * INDEX_ROWS, rank), BF16, True)],
        [],
        [gain, base, next_read, parent_rows],
        2 * (vectors + rank) * panel * rank,
    )
    if chips <= 2:
        block, held = lax.optimization_barrier((block, held))
        prior = flipped(block, 2)
        swap = swapped(held, 4)
    other = flipped(block, 1)
    hop_outs = [
        ((vectors, rank), F32, True),
        ((top_rows, rank), BF16, True),
        ((rank, rank), BF16, True),
    ]
    outs = [
        ((vectors, panel), F32, True),
        ((top_rows, rank), BF16, True),
        ((rank, panel), BF16, True),
    ] + hop_outs * (chips > 2)
    fixed, reach, slope, *hops = kernel_call(
        chain_kernel, outs, [], [gain, base, block, other], CHAIN_COST
    )

    (top,) = kernel_call(
        functools.partial(last_kernel, levels - 1),
        [((rows, top_rows), BF16, True)],
        [],
        [own, cross, held, swap],
        LEVEL_COST if chips > 2 else LAST_COST,
    )
    slabs = [top] + [flipped(top, mask) for mask in range(1, chain)]
    wide = pltpu.VMEM((vectors, top_rows), F32)
    staging = [pltpu.VMEM((vectors, panel), BF16), pltpu.SemaphoreType.DMA((4,))]
    results = [((vectors, panel), BF16, False), ((rows, top_rows), BF16, False)]
    if chips <= 2:
        prior, _ = lax.optimization_barrier((prior, top))
        prior_maps = kernel_call(
            prior_kernel, hop_outs[:2], [], [prior, flipped(prior, 1)], PRIOR_COST
        )
        solved, top = kernel_call(
            whole_kernel,
            results,
            [wide, *staging, pltpu.SemaphoreType.DMA],
            [fixed, reach, gain, slope, *prior_maps, *slabs],
        )
        return (top, solved)

    hop_fixed, hop, hop_slope = hops
    whole, passed = kernel_call(
        pass_kernel,
        [((vectors, top_rows), BF16, True), ((vectors, rank), BF16, True)],
        [wide],
        [hop_fixed, hop, *slabs],
    )
    start = passed
    for _ in range(chips - 2):
        here = jnp.where(lax.axis_index("fr") >= 2, turned(passed, 2), 0)
        passed = (start.astype(F32) + dot(here, hop_slope)).astype(BF16)
    arrived = turned(passed, 2)
    ready, solved, top = kernel_call(
        link_kernel,
        [((vectors, panel), F32, True), *results],
        [*staging, pltpu.SemaphoreType.DMA],
        [fixed, reach, gain, whole, top],
    )
    (solved,) = kernel_call(
        final_kernel,
        [((vectors, panel), BF16, False)],
        staging,
        [ready, slope, arrived],
        remote=[solved],
        aliases={3: 0},
    )
    return (top, solved)


def solution(mesh):
    placed = (
        P("fr", "bf"),
        P(None, "bf", None),
        P(None, "bf", None),
        P(None, "bf", None),
        P(("bf", "fr"), None),
        P(None, ("bf", "fr")),
        P(("bf", "fr"), None),
        P(("bf", "fr"), None),
        P(("bf", "fr"), None),
    )
    return jax.shard_map(
        body,
        mesh=mesh,
        in_specs=placed,
        out_specs=(P("fr", "bf"), P(None, ("bf", "fr"))),
        check_vma=False,
    )
```

```python
import functools

import jax
import jax.numpy as jnp
from jax import lax
from jax.experimental import pallas as pl
from jax.experimental.pallas import tpu as pltpu
from jax.sharding import PartitionSpec as P

BF16 = jnp.bfloat16
F32 = jnp.float32
LOW_BITS = 8
INDEX_ROWS = 16
PANEL_COST = 10**9
CHAIN_COST = 3 * 10**9
PRIOR_COST = 10**9
BLOCK_COST = 10**9
LAST_COST = 10**8
LEVEL_COST = 2 * 10**9

def dot(left, right):
    return jnp.dot(left, right, preferred_element_type=F32)


def picker(columns, size):
    rows = lax.broadcasted_iota(jnp.int32, (size, columns.shape[1]), 0)
    return jnp.where(rows == columns, 1.0, 0.0).astype(BF16)


def kernel_call(kernel, outs, scratch, operands, flops=0, remote=(), aliases=None):
    vmem, hbm = pl.BlockSpec(memory_space=pltpu.VMEM), pl.BlockSpec(memory_space=pltpu.HBM)
    shapes = [
        pltpu.VMEM(shape, dtype) if inside else jax.ShapeDtypeStruct(shape, dtype)
        for shape, dtype, inside in outs
    ]
    placed = [pltpu.with_memory_space_constraint(x, pltpu.VMEM) for x in operands]
    return pl.pallas_call(
        kernel,
        out_shape=shapes,
        in_specs=[vmem] * len(placed) + [hbm] * len(remote),
        out_specs=[vmem if inside else hbm for _, _, inside in outs],
        scratch_shapes=scratch,
        compiler_params=pltpu.CompilerParams(vmem_limit_bytes=24 * 1024 * 1024),
        input_output_aliases=aliases or {},
        cost_estimate=pl.CostEstimate(flops=flops, bytes_accessed=0, transcendentals=0),
    )(*placed, *[pltpu.with_memory_space_constraint(x, pltpu.HBM) for x in remote])


def shuffle_kernel(source_hbm, order_hbm, out_ref, order_ref, source, sems):
    copies = [
        pltpu.make_async_copy(order_hbm, order_ref, sems.at[0]),
        pltpu.make_async_copy(source_hbm, source, sems.at[1]),
    ]
    for copy in copies:
        copy.start()
    copies[0].wait()
    pick = picker(order_ref[0], source.shape[1])
    copies[1].wait()
    out_ref[...] = dot(source[...], pick).astype(BF16)


def fold(factor, pick):
    size = factor.shape[0]
    pieces = [dot(factor, pick[start : start + size]) for start in range(0, pick.shape[0], size)]
    return jnp.concatenate(pieces, axis=0).astype(BF16)


def ready_kernel(
    order_ref, held_ref, own_hbm, cross_hbm, rows_hbm, write_hbm, source_hbm, inverse_hbm,
    part_ref, fold_ref, own_ref, cross_ref, rows_ref, left_ref, inverse_ref, sems,
):
    rank, size = write_hbm.shape
    pairs = [
        (own_hbm, own_ref),
        (cross_hbm, cross_ref),
        (rows_hbm, rows_ref),
        (write_hbm, left_ref.at[:rank]),
        (source_hbm, left_ref.at[rank:]),
    ]
    for start in range(0, size, rank):
        block = (pl.ds(start, rank), pl.ds(0, start + rank))
        pairs.append((inverse_hbm.at[block], inverse_ref.at[block]))
    copies = [pltpu.make_async_copy(a, b, sems.at[i]) for i, (a, b) in enumerate(pairs)]
    for copy in copies:
        copy.start()
    pick = picker(order_ref[1], held_ref.shape[1])
    for copy in copies[:2]:
        copy.wait()
    part_ref[...] = dot(held_ref[...], fold(own_ref[0], pick))
    fold_ref[...] = fold(cross_ref[0], pick)
    for copy in copies[2:]:
        copy.wait()


def panel_kernel(
    level, order_ref, held_ref, own_ref, cross_ref, left_ref, inverse_ref, part_ref, fold_ref, gain_ref, base_ref
):
    rank, size = gain_ref.shape
    pick = picker(order_ref[level + 1], held_ref.shape[1])
    part_ref[...] = dot(held_ref[...], fold(own_ref[level], pick))
    fold_ref[...] = fold(cross_ref[level], pick)
    for start in range(0, size, rank):
        cut = slice(start, start + rank)
        product = dot(left_ref[:, start:], inverse_ref[start:, cut])
        gain_ref[:, cut] = product[:rank].astype(BF16)
        base_ref[:, cut] = product[rank:]


def block_kernel(gain_ref, base_ref, read_ref, rows_ref, block_ref):
    vectors, rank = base_ref.shape[0], gain_ref.shape[0]
    read = read_ref[...]
    block_ref[:vectors] = dot(base_ref[...].astype(BF16), read).astype(BF16)
    block_ref[vectors : vectors + rank] = dot(gain_ref[...], read).astype(BF16)
    rows = rows_ref[...]
    low = jnp.bitwise_and(rows, 2**LOW_BITS - 1)
    high = lax.shift_right_logical(rows, jnp.full(rows.shape, LOW_BITS, jnp.int32))
    at = vectors + rank
    for part in (low, high):
        wide = jnp.broadcast_to(part.astype(F32), (INDEX_ROWS, rank))
        block_ref[at : at + INDEX_ROWS] = wide.astype(BF16)
        at += INDEX_ROWS


def mixed(own_part, partner_part, own, cross):
    size = own.shape[0]
    pieces = []
    for start in range(0, own_part.shape[1], size):
        cut = slice(start, start + size)
        pieces.append(dot(own_part[:, cut], own) + dot(partner_part[:, cut], cross))
    return jnp.concatenate(pieces, axis=1)


def level_kernel(part_ref, fold_ref, swap_ref, out_ref):
    out_ref[...] = (part_ref[...] + dot(swap_ref[...], fold_ref[...])).astype(BF16)


def pair_blocks(own_ref, other_ref, vectors, rank, top_rows):
    odd = lax.rem(lax.axis_index("fr"), 2) == 1

    def parts(ref):
        at = vectors + rank
        low = ref[at : at + INDEX_ROWS].astype(F32)[:1].astype(jnp.int32)
        at += INDEX_ROWS
        high = ref[at : at + INDEX_ROWS].astype(F32)[:1].astype(jnp.int32)
        return ref[:vectors], ref[vectors : vectors + rank], high * 2**LOW_BITS + low

    own, other = parts(own_ref), parts(other_ref)
    base_even, step_even, rows_even = (jnp.where(odd, y, x) for x, y in zip(own, other))
    base_odd, step_odd, rows_odd = (jnp.where(odd, x, y) for x, y in zip(own, other))
    pick_even, pick_odd = picker(rows_even, top_rows), picker(rows_odd, top_rows)
    past = (dot(pick_even, step_even) - pick_odd.astype(F32)).astype(BF16)
    return odd, base_even, base_odd, step_even, step_odd, pick_even, past


def chain_kernel(gain_ref, base_ref, block_ref, other_ref, fixed_ref, reach_ref, slope_ref, *hops):
    vectors, rank, top_rows = base_ref.shape[0], gain_ref.shape[0], reach_ref.shape[0]
    odd, base_even, base_odd, step_even, step_odd, pick_even, past = pair_blocks(
        block_ref, other_ref, vectors, rank, top_rows
    )
    if hops:
        hop_fixed_ref, hop_ref, hop_slope_ref = hops
        hop_fixed_ref[...] = base_odd.astype(F32) - dot(base_even, step_odd)
        hop_ref[...] = dot(past, step_odd).astype(BF16)
        hop_slope_ref[...] = dot(step_even, step_odd).astype(BF16)
    reach_ref[...] = jnp.where(odd, -past, pick_even)
    gain = gain_ref[...]
    fixed_ref[...] = base_ref[...] - dot(jnp.where(odd, base_even, jnp.zeros_like(base_even)), gain)
    slope_ref[...] = jnp.where(odd, -dot(step_even, gain), gain.astype(F32)).astype(BF16)


def prior_kernel(block_ref, other_ref, fixed_ref, reach_ref):
    (vectors, rank), top_rows = fixed_ref.shape, reach_ref.shape[0]
    _, base_even, base_odd, _, step_odd, _, past = pair_blocks(
        block_ref, other_ref, vectors, rank, top_rows
    )
    later = lax.axis_index("fr") >= 2
    fixed_ref[...] = jnp.where(later, base_odd.astype(F32) - dot(base_even, step_odd), 0.0)
    reach_ref[...] = jnp.where(later, dot(past, step_odd), 0.0).astype(BF16)


def last_kernel(level, own_ref, cross_ref, held_ref, swap_ref, top_ref):
    top_ref[...] = mixed(held_ref[...], swap_ref[...], own_ref[level], cross_ref[level]).astype(BF16)


def gathered(wide, slabs):
    rows = slabs[0].shape[0]
    place = lax.axis_index("fr")
    for flip, slab in enumerate(reversed(slabs)):
        start = pl.multiple_of(jnp.bitwise_xor(place, flip) * rows, rows)
        wide[pl.ds(start, rows), :] = slab[...].astype(F32)
    return wide[...].astype(BF16)


def pass_kernel(hop_fixed_ref, hop_ref, *refs):
    *slabs, top_ref, pass_ref, wide = refs
    top = gathered(wide, slabs)
    top_ref[...] = top
    pass_ref[...] = (hop_fixed_ref[...] + dot(top, hop_ref[...])).astype(BF16)


def written(out_hbm, held, sems, part):
    parts = sems.shape[0]
    width = held.shape[1] // parts
    copies = []
    for index in range(parts):
        cut = pl.ds(index * width, width)
        held[:, cut] = part(cut).astype(BF16)
        copies.append(pltpu.make_async_copy(held.at[:, cut], out_hbm.at[:, cut], sems.at[index]))
        copies[-1].start()
    for copy in copies:
        copy.wait()


def link_kernel(fixed_ref, reach_ref, gain_ref, whole_ref, top_ref, ready_ref, out_hbm, top_hbm, held, sems, top_sem):
    copy = pltpu.make_async_copy(top_ref, top_hbm, top_sem)
    copy.start()
    link = dot(whole_ref[...], reach_ref[...]).astype(BF16)
    ready_ref[...] = fixed_ref[...] - dot(link, gain_ref[...])

    @pl.when(lax.axis_index("fr") < 2)
    def _():
        written(out_hbm, held, sems, lambda cut: ready_ref[:, cut])

    copy.wait()


def final_kernel(ready_ref, slope_ref, arrived_ref, solved_hbm, out_hbm, held, sems):
    @pl.when(lax.axis_index("fr") >= 2)
    def _():
        arrived = arrived_ref[...]
        written(out_hbm, held, sems, lambda cut: ready_ref[:, cut] - dot(arrived, slope_ref[:, cut]))


def whole_kernel(fixed_ref, reach_ref, gain_ref, slope_ref, prior_fixed_ref, prior_ref, *refs):
    *slabs, out_hbm, top_hbm, wide, held, sems, top_sem = refs
    copy = pltpu.make_async_copy(slabs[-1], top_hbm, top_sem)
    copy.start()
    top = gathered(wide, slabs)
    link = dot(top, reach_ref[...]).astype(BF16)
    prior = (prior_fixed_ref[...] + dot(top, prior_ref[...])).astype(BF16)

    def part(cut):
        return fixed_ref[:, cut] - (dot(link, gain_ref[:, cut]) + dot(prior, slope_ref[:, cut]))

    written(out_hbm, held, sems, part)
    copy.wait()


def body(
    top_source,
    level_ordering,
    butterfly_own,
    butterfly_cross,
    parent_rows,
    front_source,
    panel_inverse,
    coupling_read,
    coupling_write,
):
    levels = level_ordering.shape[0]
    rows, top_rows = top_source.shape
    vectors, panel = front_source.shape
    rank = coupling_write.shape[0]
    groups, chain = lax.axis_size("bf"), lax.axis_size("fr")
    chips = chain // 2

    def flipped(array, mask):
        return lax.ppermute(array, "fr", [(i, i ^ mask) for i in range(chain)])

    def turned(array, by):
        return lax.ppermute(array, "fr", [(i, (i + by) % chain) for i in range(chain)])

    def swapped(array, mask):
        return lax.ppermute(array, "bf", [(g, g ^ mask) for g in range(groups)])

    held, order = kernel_call(
        shuffle_kernel,
        [((rows, top_rows), BF16, True), (level_ordering.shape, jnp.int32, True)],
        [pltpu.VMEM((rows, top_rows), BF16), pltpu.SemaphoreType.DMA((2,))],
        [],
        remote=[top_source, level_ordering],
    )
    swap = swapped(held, 1)
    if chips > 2:
        coupling_read, order = lax.optimization_barrier((coupling_read, order))
    next_read = turned(coupling_read, -1)
    ready_outs = [((rows, top_rows), F32, True), ((top_rows, top_rows), BF16, True)]
    part, folded, own, cross, parent_rows, left, inverse = kernel_call(
        ready_kernel,
        [
            *ready_outs,
            (butterfly_own.shape, BF16, True),
            (butterfly_cross.shape, BF16, True),
            (parent_rows.shape, jnp.int32, True),
            ((rank + vectors, panel), BF16, True),
            (panel_inverse.shape, BF16, True),
        ],
        [pltpu.SemaphoreType.DMA((5 + panel // rank,))],
        [order, held],
        remote=[
            butterfly_own, butterfly_cross, parent_rows, coupling_write, front_source, panel_inverse
        ],
    )

    def next_level(part, folded, swap):
        return kernel_call(
            level_kernel, [((rows, top_rows), BF16, True)], [], [part, folded, swap], LEVEL_COST
        )[0]

    held = next_level(part, folded, swap)
    swap = swapped(held, 2)
    part, folded, gain, base = kernel_call(
        functools.partial(panel_kernel, 1),
        [*ready_outs, ((rank, panel), BF16, True), ((vectors, panel), F32, True)],
        [],
        [order, held, own, cross, left, inverse],
        PANEL_COST,
    )

    def products(next_read):
        return kernel_call(
            block_kernel,
            [((vectors + rank + 2 * INDEX_ROWS, rank), BF16, True)],
            [],
            [gain, base, next_read, parent_rows],
            BLOCK_COST,
        )[0]

    if chips <= 2:
        block = products(next_read)
        prior = flipped(block, 2)
        swap, block = lax.optimization_barrier((swap, block))
    held = next_level(part, folded, swap)
    swap = swapped(held, 4)
    if chips > 2:
        next_read, held = lax.optimization_barrier((next_read, held))
        block = products(next_read)
    other = flipped(block, 1)
    hop_outs = [
        ((vectors, rank), F32, True),
        ((top_rows, rank), BF16, True),
        ((rank, rank), BF16, True),
    ]
    outs = [
        ((vectors, panel), F32, True),
        ((top_rows, rank), BF16, True),
        ((rank, panel), BF16, True),
    ] + hop_outs * (chips > 2)
    fixed, reach, slope, *hops = kernel_call(
        chain_kernel, outs, [], [gain, base, block, other], CHAIN_COST
    )

    (top,) = kernel_call(
        functools.partial(last_kernel, levels - 1),
        [((rows, top_rows), BF16, True)],
        [],
        [own, cross, held, swap],
        LEVEL_COST if chips > 2 else LAST_COST,
    )
    slabs = [flipped(top, mask) for mask in range(chain - 1, 0, -1)] + [top]
    wide = pltpu.VMEM((vectors, top_rows), F32)
    staging = [pltpu.VMEM((vectors, panel), BF16), pltpu.SemaphoreType.DMA((4,))]
    results = [((vectors, panel), BF16, False), ((rows, top_rows), BF16, False)]
    if chips <= 2:
        prior, _ = lax.optimization_barrier((prior, top))
        prior_maps = kernel_call(
            prior_kernel, hop_outs[:2], [], [prior, flipped(prior, 1)], PRIOR_COST
        )
        solved, top = kernel_call(
            whole_kernel,
            results,
            [wide, *staging, pltpu.SemaphoreType.DMA],
            [fixed, reach, gain, slope, *prior_maps, *slabs],
        )
        return (top, solved)

    hop_fixed, hop, hop_slope = hops
    whole, passed = kernel_call(
        pass_kernel,
        [((vectors, top_rows), BF16, True), ((vectors, rank), BF16, True)],
        [wide],
        [hop_fixed, hop, *slabs],
    )
    start = passed
    for _ in range(chips - 2):
        here = jnp.where(lax.axis_index("fr") >= 2, turned(passed, 2), 0)
        passed = (start.astype(F32) + dot(here, hop_slope)).astype(BF16)
    arrived = turned(passed, 2)
    ready, solved, top = kernel_call(
        link_kernel,
        [((vectors, panel), F32, True), *results],
        [*staging, pltpu.SemaphoreType.DMA],
        [fixed, reach, gain, whole, top],
    )
    (solved,) = kernel_call(
        final_kernel,
        [((vectors, panel), BF16, False)],
        staging,
        [ready, slope, arrived],
        remote=[solved],
        aliases={3: 0},
    )
    return (top, solved)


def solution(mesh):
    placed = (
        P("fr", "bf"),
        P(None, "bf", None),
        P(None, "bf", None),
        P(None, "bf", None),
        P(("bf", "fr"), None),
        P(None, ("bf", "fr")),
        P(("bf", "fr"), None),
        P(("bf", "fr"), None),
        P(("bf", "fr"), None),
    )
    return jax.shard_map(
        body,
        mesh=mesh,
        in_specs=placed,
        out_specs=(P("fr", "bf"), P(None, ("bf", "fr"))),
        check_vma=False,
    )
```

```python
import functools

import jax
import jax.numpy as jnp
from jax import lax
from jax.experimental import pallas as pl
from jax.experimental.pallas import tpu as pltpu
from jax.sharding import PartitionSpec as P

BF16 = jnp.bfloat16
F32 = jnp.float32
LOW_BITS = 8
INDEX_ROWS = 16
PANEL_COST = 10**9
CHAIN_COST = 3 * 10**9
PRIOR_COST = 10**9
BLOCK_COST = 10**9
LAST_COST = 10**8
LEVEL_COST = 2 * 10**9

def dot(left, right):
    return jnp.dot(left, right, preferred_element_type=F32)


def picker(columns, size):
    rows = lax.broadcasted_iota(jnp.int32, (size, columns.shape[1]), 0)
    return jnp.where(rows == columns, 1.0, 0.0).astype(BF16)


def kernel_call(kernel, outs, scratch, operands, flops=0, remote=(), aliases=None):
    vmem, hbm = pl.BlockSpec(memory_space=pltpu.VMEM), pl.BlockSpec(memory_space=pltpu.HBM)
    shapes = [
        pltpu.VMEM(shape, dtype) if inside else jax.ShapeDtypeStruct(shape, dtype)
        for shape, dtype, inside in outs
    ]
    placed = [pltpu.with_memory_space_constraint(x, pltpu.VMEM) for x in operands]
    return pl.pallas_call(
        kernel,
        out_shape=shapes,
        in_specs=[vmem] * len(placed) + [hbm] * len(remote),
        out_specs=[vmem if inside else hbm for _, _, inside in outs],
        scratch_shapes=scratch,
        compiler_params=pltpu.CompilerParams(vmem_limit_bytes=24 * 1024 * 1024),
        input_output_aliases=aliases or {},
        cost_estimate=pl.CostEstimate(flops=flops, bytes_accessed=0, transcendentals=0),
    )(*placed, *[pltpu.with_memory_space_constraint(x, pltpu.HBM) for x in remote])


def shuffle_kernel(source_hbm, order_hbm, out_ref, order_ref, source, sems):
    copies = [
        pltpu.make_async_copy(order_hbm, order_ref, sems.at[0]),
        pltpu.make_async_copy(source_hbm, source, sems.at[1]),
    ]
    for copy in copies:
        copy.start()
    copies[0].wait()
    pick = picker(order_ref[0], source.shape[1])
    copies[1].wait()
    out_ref[...] = dot(source[...], pick).astype(BF16)


def fold(factor, pick):
    size = factor.shape[0]
    pieces = [dot(factor, pick[start : start + size]) for start in range(0, pick.shape[0], size)]
    return jnp.concatenate(pieces, axis=0).astype(BF16)


def ready_kernel(
    order_ref, held_ref, own_hbm, cross_hbm, rows_hbm, write_hbm, source_hbm, inverse_hbm,
    part_ref, fold_ref, next_own_ref, next_fold_ref, own_ref, cross_ref, rows_ref, left_ref, inverse_ref, sems,
):
    rank, size = write_hbm.shape
    pairs = [
        (own_hbm, own_ref),
        (cross_hbm, cross_ref),
        (rows_hbm, rows_ref),
        (write_hbm, left_ref.at[:rank]),
        (source_hbm, left_ref.at[rank:]),
    ]
    for start in range(0, size, rank):
        block = (pl.ds(start, rank), pl.ds(0, start + rank))
        pairs.append((inverse_hbm.at[block], inverse_ref.at[block]))
    copies = [pltpu.make_async_copy(a, b, sems.at[i]) for i, (a, b) in enumerate(pairs)]
    for copy in copies:
        copy.start()
    pick = picker(order_ref[1], held_ref.shape[1])
    for copy in copies[:2]:
        copy.wait()
    part_ref[...] = dot(held_ref[...], fold(own_ref[0], pick))
    fold_ref[...] = fold(cross_ref[0], pick)
    pick = picker(order_ref[2], held_ref.shape[1])
    next_own_ref[...] = fold(own_ref[1], pick)
    next_fold_ref[...] = fold(cross_ref[1], pick)
    for copy in copies[2:]:
        copy.wait()


def panel_kernel(held_ref, fold_ref, left_ref, inverse_ref, part_ref, gain_ref, base_ref):
    rank, size = gain_ref.shape
    part_ref[...] = dot(held_ref[...], fold_ref[...])
    for start in range(0, size, rank):
        cut = slice(start, start + rank)
        product = dot(left_ref[:, start:], inverse_ref[start:, cut])
        gain_ref[:, cut] = product[:rank].astype(BF16)
        base_ref[:, cut] = product[rank:]


def block_kernel(gain_ref, base_ref, read_ref, rows_ref, block_ref):
    vectors, rank = base_ref.shape[0], gain_ref.shape[0]
    read = read_ref[...]
    block_ref[:vectors] = dot(base_ref[...].astype(BF16), read).astype(BF16)
    block_ref[vectors : vectors + rank] = dot(gain_ref[...], read).astype(BF16)
    rows = rows_ref[...]
    low = jnp.bitwise_and(rows, 2**LOW_BITS - 1)
    high = lax.shift_right_logical(rows, jnp.full(rows.shape, LOW_BITS, jnp.int32))
    at = vectors + rank
    for part in (low, high):
        wide = jnp.broadcast_to(part.astype(F32), (INDEX_ROWS, rank))
        block_ref[at : at + INDEX_ROWS] = wide.astype(BF16)
        at += INDEX_ROWS


def mixed(own_part, partner_part, own, cross):
    size = own.shape[0]
    pieces = []
    for start in range(0, own_part.shape[1], size):
        cut = slice(start, start + size)
        pieces.append(dot(own_part[:, cut], own) + dot(partner_part[:, cut], cross))
    return jnp.concatenate(pieces, axis=1)


def level_kernel(part_ref, fold_ref, swap_ref, out_ref):
    out_ref[...] = (part_ref[...] + dot(swap_ref[...], fold_ref[...])).astype(BF16)


def pair_blocks(own_ref, other_ref, vectors, rank, top_rows):
    odd = lax.rem(lax.axis_index("fr"), 2) == 1

    def parts(ref):
        at = vectors + rank
        low = ref[at : at + INDEX_ROWS].astype(F32)[:1].astype(jnp.int32)
        at += INDEX_ROWS
        high = ref[at : at + INDEX_ROWS].astype(F32)[:1].astype(jnp.int32)
        return ref[:vectors], ref[vectors : vectors + rank], high * 2**LOW_BITS + low

    own, other = parts(own_ref), parts(other_ref)
    base_even, step_even, rows_even = (jnp.where(odd, y, x) for x, y in zip(own, other))
    base_odd, step_odd, rows_odd = (jnp.where(odd, x, y) for x, y in zip(own, other))
    pick_even, pick_odd = picker(rows_even, top_rows), picker(rows_odd, top_rows)
    past = (dot(pick_even, step_even) - pick_odd.astype(F32)).astype(BF16)
    return odd, base_even, base_odd, step_even, step_odd, pick_even, past


def chain_kernel(gain_ref, base_ref, block_ref, other_ref, fixed_ref, reach_ref, slope_ref, *hops):
    vectors, rank, top_rows = base_ref.shape[0], gain_ref.shape[0], reach_ref.shape[0]
    odd, base_even, base_odd, step_even, step_odd, pick_even, past = pair_blocks(
        block_ref, other_ref, vectors, rank, top_rows
    )
    if hops:
        hop_fixed_ref, hop_ref, hop_slope_ref = hops
        hop_fixed_ref[...] = base_odd.astype(F32) - dot(base_even, step_odd)
        hop_ref[...] = dot(past, step_odd).astype(BF16)
        hop_slope_ref[...] = dot(step_even, step_odd).astype(BF16)
    reach_ref[...] = jnp.where(odd, -past, pick_even)
    gain = gain_ref[...]
    fixed_ref[...] = base_ref[...] - dot(jnp.where(odd, base_even, jnp.zeros_like(base_even)), gain)
    slope_ref[...] = jnp.where(odd, -dot(step_even, gain), gain.astype(F32)).astype(BF16)


def prior_kernel(block_ref, other_ref, fixed_ref, reach_ref):
    (vectors, rank), top_rows = fixed_ref.shape, reach_ref.shape[0]
    _, base_even, base_odd, _, step_odd, _, past = pair_blocks(
        block_ref, other_ref, vectors, rank, top_rows
    )
    later = lax.axis_index("fr") >= 2
    fixed_ref[...] = jnp.where(later, base_odd.astype(F32) - dot(base_even, step_odd), 0.0)
    reach_ref[...] = jnp.where(later, dot(past, step_odd), 0.0).astype(BF16)


def last_kernel(level, own_ref, cross_ref, held_ref, swap_ref, top_ref):
    top_ref[...] = mixed(held_ref[...], swap_ref[...], own_ref[level], cross_ref[level]).astype(BF16)


def gathered(wide, slabs):
    rows = slabs[0].shape[0]
    place = lax.axis_index("fr")
    for flip, slab in enumerate(reversed(slabs)):
        start = pl.multiple_of(jnp.bitwise_xor(place, flip) * rows, rows)
        wide[pl.ds(start, rows), :] = slab[...].astype(F32)
    return wide[...].astype(BF16)


def pass_kernel(hop_fixed_ref, hop_ref, *refs):
    *slabs, top_ref, pass_ref, wide = refs
    top = gathered(wide, slabs)
    top_ref[...] = top
    pass_ref[...] = (hop_fixed_ref[...] + dot(top, hop_ref[...])).astype(BF16)


def written(out_hbm, held, sems, part):
    parts = sems.shape[0]
    width = held.shape[1] // parts
    copies = []
    for index in range(parts):
        cut = pl.ds(index * width, width)
        held[:, cut] = part(cut).astype(BF16)
        copies.append(pltpu.make_async_copy(held.at[:, cut], out_hbm.at[:, cut], sems.at[index]))
        copies[-1].start()
    for copy in copies:
        copy.wait()


def link_kernel(fixed_ref, reach_ref, gain_ref, whole_ref, top_ref, ready_ref, out_hbm, top_hbm, held, sems, top_sem):
    copy = pltpu.make_async_copy(top_ref, top_hbm, top_sem)
    copy.start()
    link = dot(whole_ref[...], reach_ref[...]).astype(BF16)
    ready_ref[...] = fixed_ref[...] - dot(link, gain_ref[...])

    @pl.when(lax.axis_index("fr") < 2)
    def _():
        written(out_hbm, held, sems, lambda cut: ready_ref[:, cut])

    copy.wait()


def final_kernel(ready_ref, slope_ref, arrived_ref, solved_hbm, out_hbm, held, sems):
    @pl.when(lax.axis_index("fr") >= 2)
    def _():
        arrived = arrived_ref[...]
        written(out_hbm, held, sems, lambda cut: ready_ref[:, cut] - dot(arrived, slope_ref[:, cut]))


def whole_kernel(fixed_ref, reach_ref, gain_ref, slope_ref, prior_fixed_ref, prior_ref, *refs):
    *slabs, out_hbm, top_hbm, wide, held, sems, top_sem = refs
    copy = pltpu.make_async_copy(slabs[-1], top_hbm, top_sem)
    copy.start()
    top = gathered(wide, slabs)
    link = dot(top, reach_ref[...]).astype(BF16)
    prior = (prior_fixed_ref[...] + dot(top, prior_ref[...])).astype(BF16)

    def part(cut):
        return fixed_ref[:, cut] - (dot(link, gain_ref[:, cut]) + dot(prior, slope_ref[:, cut]))

    written(out_hbm, held, sems, part)
    copy.wait()


def body(
    top_source,
    level_ordering,
    butterfly_own,
    butterfly_cross,
    parent_rows,
    front_source,
    panel_inverse,
    coupling_read,
    coupling_write,
):
    levels = level_ordering.shape[0]
    rows, top_rows = top_source.shape
    vectors, panel = front_source.shape
    rank = coupling_write.shape[0]
    groups, chain = lax.axis_size("bf"), lax.axis_size("fr")
    chips = chain // 2

    def flipped(array, mask):
        return lax.ppermute(array, "fr", [(i, i ^ mask) for i in range(chain)])

    def turned(array, by):
        return lax.ppermute(array, "fr", [(i, (i + by) % chain) for i in range(chain)])

    def swapped(array, mask):
        return lax.ppermute(array, "bf", [(g, g ^ mask) for g in range(groups)])

    held, order = kernel_call(
        shuffle_kernel,
        [((rows, top_rows), BF16, True), (level_ordering.shape, jnp.int32, True)],
        [pltpu.VMEM((rows, top_rows), BF16), pltpu.SemaphoreType.DMA((2,))],
        [],
        remote=[top_source, level_ordering],
    )
    swap = swapped(held, 1)
    if chips > 2:
        coupling_read, order = lax.optimization_barrier((coupling_read, order))
    next_read = turned(coupling_read, -1)
    ready_outs = [((rows, top_rows), F32, True), ((top_rows, top_rows), BF16, True)]
    part, folded, next_own, next_folded, own, cross, parent_rows, left, inverse = kernel_call(
        ready_kernel,
        [
            *ready_outs,
            ready_outs[1],
            ready_outs[1],
            (butterfly_own.shape, BF16, True),
            (butterfly_cross.shape, BF16, True),
            (parent_rows.shape, jnp.int32, True),
            ((rank + vectors, panel), BF16, True),
            (panel_inverse.shape, BF16, True),
        ],
        [pltpu.SemaphoreType.DMA((5 + panel // rank,))],
        [order, held],
        remote=[
            butterfly_own, butterfly_cross, parent_rows, coupling_write, front_source, panel_inverse
        ],
    )

    def next_level(part, folded, swap):
        return kernel_call(
            level_kernel, [((rows, top_rows), BF16, True)], [], [part, folded, swap], LEVEL_COST
        )[0]

    held = next_level(part, folded, swap)
    swap = swapped(held, 2)
    part, gain, base = kernel_call(
        panel_kernel,
        [ready_outs[0], ((rank, panel), BF16, True), ((vectors, panel), F32, True)],
        [],
        [held, next_own, left, inverse],
        PANEL_COST,
    )

    def products(next_read):
        return kernel_call(
            block_kernel,
            [((vectors + rank + 2 * INDEX_ROWS, rank), BF16, True)],
            [],
            [gain, base, next_read, parent_rows],
            BLOCK_COST,
        )[0]

    if chips <= 2:
        block = products(next_read)
        prior, other = flipped(block, 2), flipped(block, 1)
        swap, block = lax.optimization_barrier((swap, block))
    held = next_level(part, next_folded, swap)
    swap = swapped(held, 4)
    if chips > 2:
        next_read, held = lax.optimization_barrier((next_read, held))
        block = products(next_read)
    if chips > 2:
        other = flipped(block, 1)
    hop_outs = [
        ((vectors, rank), F32, True),
        ((top_rows, rank), BF16, True),
        ((rank, rank), BF16, True),
    ]
    outs = [
        ((vectors, panel), F32, True),
        ((top_rows, rank), BF16, True),
        ((rank, panel), BF16, True),
    ] + hop_outs * (chips > 2)
    fixed, reach, slope, *hops = kernel_call(
        chain_kernel, outs, [], [gain, base, block, other], CHAIN_COST
    )

    (top,) = kernel_call(
        functools.partial(last_kernel, levels - 1),
        [((rows, top_rows), BF16, True)],
        [],
        [own, cross, held, swap],
        LEVEL_COST if chips > 2 else LAST_COST,
    )
    slabs = [flipped(top, mask) for mask in range(chain - 1, 0, -1)] + [top]
    wide = pltpu.VMEM((vectors, top_rows), F32)
    staging = [pltpu.VMEM((vectors, panel), BF16), pltpu.SemaphoreType.DMA((4,))]
    results = [((vectors, panel), BF16, False), ((rows, top_rows), BF16, False)]
    if chips <= 2:
        prior, _ = lax.optimization_barrier((prior, top))
        prior_maps = kernel_call(
            prior_kernel, hop_outs[:2], [], [prior, flipped(prior, 1)], PRIOR_COST
        )
        solved, top = kernel_call(
            whole_kernel,
            results,
            [wide, *staging, pltpu.SemaphoreType.DMA],
            [fixed, reach, gain, slope, *prior_maps, *slabs],
        )
        return (top, solved)

    hop_fixed, hop, hop_slope = hops
    whole, passed = kernel_call(
        pass_kernel,
        [((vectors, top_rows), BF16, True), ((vectors, rank), BF16, True)],
        [wide],
        [hop_fixed, hop, *slabs],
    )
    start = passed
    for _ in range(chips - 2):
        here = jnp.where(lax.axis_index("fr") >= 2, turned(passed, 2), 0)
        passed = (start.astype(F32) + dot(here, hop_slope)).astype(BF16)
    arrived = turned(passed, 2)
    ready, solved, top = kernel_call(
        link_kernel,
        [((vectors, panel), F32, True), *results],
        [*staging, pltpu.SemaphoreType.DMA],
        [fixed, reach, gain, whole, top],
    )
    (solved,) = kernel_call(
        final_kernel,
        [((vectors, panel), BF16, False)],
        staging,
        [ready, slope, arrived],
        remote=[solved],
        aliases={3: 0},
    )
    return (top, solved)


def solution(mesh):
    placed = (
        P("fr", "bf"),
        P(None, "bf", None),
        P(None, "bf", None),
        P(None, "bf", None),
        P(("bf", "fr"), None),
        P(None, ("bf", "fr")),
        P(("bf", "fr"), None),
        P(("bf", "fr"), None),
        P(("bf", "fr"), None),
    )
    return jax.shard_map(
        body,
        mesh=mesh,
        in_specs=placed,
        out_specs=(P("fr", "bf"), P(None, ("bf", "fr"))),
        check_vma=False,
    )
```
